128 devices in a mesh: grp: 2 (over x_lo), row: 8 (over y, core), col: 8 (over x_hi, z).
Axes of the slice: x: 4 (x_hi: 2, x_lo: 2; x = x_hi * 2 + x_lo), y: 4, z: 4, core: 2. Of those that a mesh axis runs over, the one named last changes fastest.
Arguments:
- teacher_image: bfloat16 [16384, 1024], P(('grp', 'row', 'col')), may hold values from -4 to 4
- student_image: bfloat16 [16384, 512], P(('grp', 'row', 'col')), may hold values from -4 to 4
- teacher_text: bfloat16 [16384, 1024], P(('grp', 'row', 'col')), may hold values from -4 to 4
- student_text: bfloat16 [16384, 512], P(('grp', 'row', 'col')), may hold values from -4 to 4
Outputs:
- grad_student_image: float32 [16384, 512], P(('grp', 'row', 'col'))
- grad_student_text: float32 [16384, 512], P(('grp', 'row', 'col'))
The draws below stay inside these ranges and needn't reach their ends.
All inputs are finite; a program needn't handle non-finite values.
Results may differ from the reference program's by a relative error of at most 0.0071.
Values may be sent and summed in bfloat16 or wider, within the bound.
A program may use at most 64 MiB of HBM per device.

```python
import math
import jax
import jax.numpy as jnp
import numpy as np
from jax import lax

TEACHER_DIM = 1024
STUDENT_DIM = 512
PAIRS = 16384


def group_ids(key):
    total = 256
    weights = 1.0 / np.arange(1, total + 1)
    bounds = np.floor(np.cumsum(weights) / np.sum(weights) * 1048576.0).astype(np.int32)
    first, second = jax.random.split(key)
    ticket = jax.random.randint(first, (PAIRS, 1), 0, 1048576, jnp.int32)
    ranked = jnp.sum((ticket >= jnp.asarray(bounds)[None, :]).astype(jnp.int32), axis=1)
    ranked = jnp.minimum(ranked, total - 1)
    order = jax.random.permutation(second, total)
    return jnp.take(order, ranked)


def shared_base(key, width, model_tag):
    labels = group_ids(jax.random.fold_in(key, 303))
    centers = jax.random.truncated_normal(jax.random.fold_in(key, model_tag), -4.0, 4.0, (256, width), jnp.float32)
    noise = jax.random.truncated_normal(jax.random.fold_in(key, model_tag + 1), -4.0, 4.0, (PAIRS, width), jnp.float32)
    return jnp.take(centers, labels, axis=0) + noise


def row_scales(key, low, high):
    return jnp.exp(jax.random.uniform(key, (PAIRS, 1), jnp.float32, math.log(low), math.log(high)))


def finish(base, key, width, spread):
    first, second = jax.random.split(key)
    extra = jax.random.truncated_normal(first, -4.0, 4.0, (PAIRS, width), jnp.float32)
    scales = row_scales(second, 1.0, 10.0)
    values = (base + spread * extra) * scales / math.sqrt(width)
    return jnp.clip(values, -4.0, 4.0).astype(jnp.bfloat16)


def draw_teacher_image(key, part):
    base = shared_base(key, TEACHER_DIM, 101)
    key = jax.random.fold_in(key, 1)
    return finish(base, key, TEACHER_DIM, 0.3)


def draw_teacher_text(key, part):
    base = shared_base(key, TEACHER_DIM, 101)
    key = jax.random.fold_in(key, 2)
    return finish(base, key, TEACHER_DIM, 0.5)


def draw_student_image(key, part):
    base = shared_base(key, STUDENT_DIM, 202)
    key = jax.random.fold_in(key, 3)
    return finish(base, key, STUDENT_DIM, 0.8)


def draw_student_text(key, part):
    base = shared_base(key, STUDENT_DIM, 202)
    key = jax.random.fold_in(key, 4)
    return finish(base, key, STUDENT_DIM, 0.8)


def setup_inputs(seed: int = 0) -> dict:
    key_of = jax.random.split(jax.random.key(seed), 5)
    teacher_image = draw_teacher_image(jax.random.fold_in(key_of[4], 71), 0)
    student_image = draw_student_image(jax.random.fold_in(key_of[4], 71), 0)
    teacher_text = draw_teacher_text(jax.random.fold_in(key_of[4], 71), 0)
    student_text = draw_student_text(jax.random.fold_in(key_of[4], 71), 0)
    return {"teacher_image": teacher_image, "student_image": student_image, "teacher_text": teacher_text, "student_text": student_text}


EPS = 1e-06
LOGIT_SCALE = 14.285714285714286

def unit_rows(raw):
    values = raw.astype(jnp.float32)
    inverse = lax.rsqrt(lax.optimization_barrier(jnp.sum(values * values, axis=1, keepdims=True)) + EPS)
    return (values * inverse, inverse)

def logits(left, right):
    return LOGIT_SCALE * jnp.dot(left, right.T, preferred_element_type=jnp.float32)

def reference(teacher_image, student_image, teacher_text, student_text):
    norm_si, inv_si = unit_rows(student_image)
    norm_st, inv_st = unit_rows(student_text)
    norm_ti, inv_ti = unit_rows(teacher_image)
    norm_tt, inv_tt = unit_rows(teacher_text)
    unit_si = norm_si.astype(jnp.bfloat16)
    unit_st = norm_st.astype(jnp.bfloat16)
    unit_ti = norm_ti.astype(jnp.bfloat16)
    unit_tt = norm_tt.astype(jnp.bfloat16)
    block = min(512, PAIRS)
    count = PAIRS // block
    stud_blocks = unit_si.reshape(count, block, unit_si.shape[1])
    teach_blocks = unit_ti.reshape(count, block, unit_ti.shape[1])

    def first_pass(carry, pieces):
        exp_student = jnp.exp(logits(pieces[0], unit_st))
        exp_teacher = jnp.exp(logits(pieces[1], unit_tt))
        new_carry = (carry[0] + lax.optimization_barrier(jnp.sum(exp_student, axis=0)), carry[1] + lax.optimization_barrier(jnp.sum(exp_teacher, axis=0)))
        return (new_carry, (lax.optimization_barrier(jnp.sum(exp_student, axis=1)), lax.optimization_barrier(jnp.sum(exp_teacher, axis=1))))
    zero_cols = jnp.zeros((PAIRS,), jnp.float32)
    col_sums, row_sums = lax.scan(first_pass, (zero_cols, zero_cols), (stud_blocks, teach_blocks))
    inv_cs = 1.0 / col_sums[0]
    inv_ct = 1.0 / col_sums[1]
    inv_rs = 1.0 / row_sums[0]
    inv_rt = 1.0 / row_sums[1]

    def second_pass(carry, pieces):
        stud_piece, teach_piece, rs_piece, rt_piece = pieces
        exp_student = jnp.exp(logits(stud_piece, unit_st))
        exp_teacher = jnp.exp(logits(teach_piece, unit_tt))
        weight = 0.5 * LOGIT_SCALE * (exp_student * (rs_piece[:, None] + inv_cs[None, :]) - exp_teacher * (rt_piece[:, None] + inv_ct[None, :]))
        weight = weight.astype(jnp.bfloat16)
        image_piece = jnp.dot(weight, unit_st, preferred_element_type=jnp.float32)
        return (carry + jnp.dot(weight.T, stud_piece, preferred_element_type=jnp.float32), image_piece)
    zero_text = jnp.zeros((PAIRS, unit_st.shape[1]), jnp.float32)
    dir_text, dir_image = lax.scan(second_pass, zero_text, (stud_blocks, teach_blocks, inv_rs, inv_rt))
    dir_image = dir_image.reshape(PAIRS, unit_si.shape[1])
    grad_image = inv_si * (dir_image - norm_si * lax.optimization_barrier(jnp.sum(norm_si * dir_image, axis=1, keepdims=True)))
    grad_text = inv_st * (dir_text - norm_st * lax.optimization_barrier(jnp.sum(norm_st * dir_text, axis=1, keepdims=True)))
    return (grad_image, grad_text)
```

```python
import jax
import jax.numpy as jnp
from jax import lax
from jax.experimental import pallas as pl
from jax.experimental.pallas import tpu as pltpu
from jax.sharding import PartitionSpec as P

EPS = 1e-06
LOGIT_SCALE = 14.285714285714286
LOG2E = 1.4426950408889634
MESH = pl.DeviceIdType.MESH
B = 128

SLOTS = [(0, 0), (0, 1), (1, 0), (3, 0), (2, 0), (1, 1), (3, 1), (2, 1)]
N = len(SLOTS)


def slot_of(step, side):
    return SLOTS.index((step % 4, side % 2))


def minus(a, b):
    return slot_of(SLOTS[a][0] - SLOTS[b][0], SLOTS[a][1] - SLOTS[b][1])


PLUS, MINUS, PAIR = (1, 0), (3, 0), (0, 1)
OWN = [(0, 1, PAIR), (0, 3, PLUS), (0, 2, MINUS)]
HOPS = [(s, d, to, piece) for piece in ("T0", "T1", "S") for s, d, to in OWN]
HOPS += [
    (3, 6, PAIR, "T0"),
    (3, 4, PLUS, "T0"),
    (2, 5, PAIR, "T1"),
    (2, 4, MINUS, "T1"),
    (3, 6, PAIR, "T1"),
    (2, 5, PAIR, "T0"),
    (3, 4, PLUS, "S0"),
    (2, 4, MINUS, "S1"),
    (1, 6, PLUS, "S"),
    (1, 5, MINUS, "S"),
    (6, 7, PLUS, "T0"),
    (5, 7, MINUS, "T1"),
    (6, 7, PLUS, "S0"),
    (5, 7, MINUS, "S1"),
]
PIECE_ROWS = {"T0": (0, 64), "T1": (64, 64), "S": (0, 128), "S0": (0, 64), "S1": (64, 64)}
N_HOPS = len(HOPS)


def dot_nt(a, b):
    return lax.dot_general(a, b, (((1,), (1,)), ((), ())), preferred_element_type=jnp.float32)


def unit_rows(raw):
    values = raw.astype(jnp.float32)
    inverse = lax.rsqrt(jnp.sum(values * values, axis=1, keepdims=True) + EPS)
    return values * inverse, inverse


def kernel(
    ti_ref, si_ref, tt_ref, st_ref, gi_ref, gt_ref,
    it, is_, xt, xs, es, et, w, ist,
    row_acc, col_acc, row_inv, col_inv,
    isum, isum_in, tsum, tsum_sib, csum, tsum_in,
    di, di_in, own_di, dt_keep, dt_other, dt_sib, dt_out, dt_in,
    hop_send, hop_recv, sib_send, sib_recv, sum_send, sum_recv, grad_send, grad_recv, grad_sib_send, grad_sib_recv,
):
    grp, row, col = lax.axis_index("grp"), lax.axis_index("row"), lax.axis_index("col")
    x_hi, z = col // 4, lax.rem(col, 4)
    y, core = row // 2, lax.rem(row, 2)

    def image_peer(step, side):
        to_grp = 1 - grp if side else grp
        return (to_grp, lax.rem(y + step, 4) * 2 + core, col)

    def text_peer(step, side):
        to_grp = 1 - grp if side else grp
        to_hi = 1 - x_hi if side else x_hi
        return (to_grp, row, to_hi * 4 + lax.rem(z + step, 4))

    peers = (image_peer, text_peer)
    sibling = (grp, y * 2 + 1 - core, col)

    barrier = pltpu.get_barrier_semaphore()
    for peer in peers:
        for slot in range(1, N):
            pl.semaphore_signal(barrier, inc=1, device_id=peer(*SLOTS[slot]), device_id_type=MESH)
    pl.semaphore_signal(barrier, inc=1, device_id=sibling, device_id_type=MESH)

    it[0:B, :] = unit_rows(ti_ref[...])[0].astype(jnp.bfloat16)
    xt[0:B, :] = unit_rows(tt_ref[...])[0].astype(jnp.bfloat16)
    is_[0:B, :] = unit_rows(si_ref[...])[0].astype(jnp.bfloat16)
    xs[0:B, :] = unit_rows(st_ref[...])[0].astype(jnp.bfloat16)

    arrays = ((it, is_, 1), (xt, xs, 2))

    def piece_ref(side, slot, piece):
        teach, stud, stride = arrays[side]
        first, rows = PIECE_ROWS[piece]
        ref = teach if piece[0] == "T" else stud
        return ref.at[pl.ds(slot * stride * B + first, rows), :]

    def hop(side, i):
        src, dst, to, piece = HOPS[i]
        return pltpu.make_async_remote_copy(
            src_ref=piece_ref(side, src, piece),
            dst_ref=piece_ref(side, dst, piece),
            send_sem=hop_send.at[side, i],
            recv_sem=hop_recv.at[side, i],
            device_id=peers[side](*to),
            device_id_type=MESH,
        )

    def start(dst, piece):
        for side in (0, 1):
            for i, h in enumerate(HOPS):
                if h[1] == dst and h[3] == piece:
                    hop(side, i).start()

    def arrived(dst, piece, sides=(0, 1)):
        for side in sides:
            for i, h in enumerate(HOPS):
                if h[1] == dst and h[3] == piece:
                    hop(side, i).wait_recv()

    def to_sibling(slot, kind):
        ref = xt if kind == "T" else xs
        k = 0 if kind == "T" else 1
        return pltpu.make_async_remote_copy(
            src_ref=ref.at[pl.ds(2 * slot * B, B), :],
            dst_ref=ref.at[pl.ds((2 * slot + 1) * B, B), :],
            send_sem=sib_send.at[k, slot],
            recv_sem=sib_recv.at[k, slot],
            device_id=sibling,
            device_id_type=MESH,
        )

    pl.semaphore_wait(barrier, 2 * (N - 1) + 1)

    for piece in ("T0", "T1", "S"):
        for dst in (1, 3, 2):
            start(dst, piece)
    to_sibling(0, "T").start()
    to_sibling(0, "S").start()

    row_acc[...] = jnp.zeros_like(row_acc)
    col_acc[...] = jnp.zeros_like(col_acc)

    def logits_tile(mat, r, c):
        left, right, out = ((is_, xs, es), (it, xt, et))[mat]
        r = pl.multiple_of(r, 512)
        c = pl.multiple_of(c, 256)
        x = dot_nt(left[pl.ds(r, 512), :], right[pl.ds(c, 256), :])
        e = jnp.exp2(x * (LOGIT_SCALE * LOG2E))
        out[pl.ds(r, 512), pl.ds(c, 256)] = e
        row_acc[mat, pl.ds(r, 512), :] += e[:, 0:128] + e[:, 128:256]
        col_acc[mat, :, pl.ds(c, 256)] += jnp.sum(e.reshape(64, 8, 256), axis=0)

    def logits(mat, rows, cols):
        n_c = (cols[1] - cols[0]) // 256
        n_r = (rows[1] - rows[0]) // 512

        def body(i, carry):
            logits_tile(mat, rows[0] + lax.rem(i, n_r) * 512, cols[0] + i // n_r * 256)
            return carry

        lax.fori_loop(0, n_c * n_r, body, 0)

    for slot in (1, 3, 2):
        arrived(slot, "T0")
    start(6, "T0")
    for i, h in enumerate(HOPS):
        if h[1] == 4 and h[3] == "T0":
            hop(0, i).start()
            hop(1, i).start()
    for slot in (2, 1, 3):
        arrived(slot, "T1")
    start(5, "T1")
    start(4, "T1")
    start(6, "T1")
    start(5, "T0")
    for slot in (1, 2, 3):
        to_sibling(slot, "T").start()
    for slot in (1, 2, 3):
        arrived(slot, "S")
    start(4, "S0")
    start(4, "S1")
    start(6, "S")
    start(5, "S")
    for slot in (1, 2, 3):
        to_sibling(slot, "S").start()
    for slot in (0, 1, 2, 3):
        to_sibling(slot, "T").wait_recv()
    logits(1, (0, 512), (0, 1024))
    for slot in (0, 1, 2, 3):
        to_sibling(slot, "S").wait_recv()
    logits(0, (0, 512), (0, 1024))
    arrived(6, "T0")
    start(7, "T0")
    arrived(5, "T1")
    start(7, "T1")
    arrived(4, "T0")
    arrived(4, "T1")
    to_sibling(4, "T").start()
    arrived(4, "S0")
    arrived(4, "S1")
    to_sibling(4, "S").start()
    arrived(6, "S")
    start(7, "S0")
    arrived(5, "S")
    start(7, "S1")
    to_sibling(5, "S").start()
    to_sibling(6, "S").start()
    to_sibling(4, "T").wait_recv()
    logits(1, (0, 512), (1024, 1280))
    to_sibling(4, "S").wait_recv()
    logits(0, (0, 512), (1024, 1280))

    for s in range(5):
        ist[:, s * B : (s + 1) * B] = is_[s * B : (s + 1) * B, :].T

    arrived(7, "T0")
    arrived(7, "T1")
    to_sibling(7, "T").start()
    arrived(6, "T1")
    to_sibling(6, "T").start()
    arrived(5, "T0")
    to_sibling(5, "T").start()
    arrived(7, "S0")
    arrived(7, "S1")
    to_sibling(7, "S").start()
    logits(1, (512, 1024), (0, 1280))
    logits(0, (512, 1024), (0, 1280))
    for slot in (5, 6, 7):
        to_sibling(slot, "T").wait_recv()
    logits(1, (0, 1024), (1280, 2048))
    for slot in (5, 6, 7):
        to_sibling(slot, "S").wait_recv()
    logits(0, (0, 1024), (1280, 2048))

    for mat in (0, 1):
        for b in range(2 * N):
            tsum[mat * 16 + b : mat * 16 + b + 1, :] = jnp.sum(
                col_acc[mat, :, b * B : (b + 1) * B], axis=0, keepdims=True
            )
    tsum_to_sib = pltpu.make_async_remote_copy(
        src_ref=tsum, dst_ref=tsum_sib, send_sem=sum_send.at[14], recv_sem=sum_recv.at[14],
        device_id=sibling, device_id_type=MESH,
    )
    tsum_to_sib.start()

    def row_total(i, carry):
        mat, s = i // N, lax.rem(i, N)
        part = row_acc[mat, pl.ds(pl.multiple_of(s * B, B), B), :]
        isum[pl.ds(i, 1), :] = jnp.sum(part.T, axis=0, keepdims=True)
        return carry

    for i in range(2 * N):
        row_total(i, 0)

    def sum_copy(side, slot):
        back = minus(0, slot) - 1
        return pltpu.make_async_remote_copy(
            src_ref=(isum, csum)[side],
            dst_ref=(isum_in, tsum_in)[side].at[back],
            send_sem=sum_send.at[side * 7 + slot - 1],
            recv_sem=sum_recv.at[side * 7 + back],
            device_id=peers[side](*SLOTS[slot]),
            device_id_type=MESH,
        )

    def sum_from(side, slot):
        return pltpu.make_async_remote_copy(
            src_ref=(isum, csum)[side],
            dst_ref=(isum_in, tsum_in)[side].at[slot - 1],
            send_sem=sum_send.at[side * 7 + slot - 1],
            recv_sem=sum_recv.at[side * 7 + slot - 1],
            device_id=peers[side](*SLOTS[slot]),
            device_id_type=MESH,
        )

    tsum_to_sib.wait_recv()
    for mat in (0, 1):
        for s in range(N):
            r = mat * 16 + 2 * s
            csum[r : r + 1, :] = tsum[r : r + 1, :] + tsum_sib[r + 1 : r + 2, :]
            csum[r + 1 : r + 2, :] = tsum[r + 1 : r + 2, :] + tsum_sib[r : r + 1, :]
    for slot in range(N - 1, 0, -1):
        sum_copy(1, slot).start()
    for slot in range(N - 1, 0, -1):
        sum_copy(0, slot).start()

    for s in range(5, N):
        ist[:, s * B : (s + 1) * B] = is_[s * B : (s + 1) * B, :].T

    for slot in range(1, N):
        sum_from(0, slot).wait_recv()
    half = 0.5 * LOGIT_SCALE
    for mat in (0, 1):
        for t in range(N):
            total = isum[mat * N + t : mat * N + t + 1, :]
            for e in range(1, N):
                r = mat * N + minus(t, e)
                total = total + isum_in[e - 1, r : r + 1, :]
            row_inv[mat, t * B : (t + 1) * B, :] = jnp.broadcast_to(half / total, (B, B)).T
    for slot in range(1, N):
        sum_from(1, slot).wait_recv()
    for mat in (0, 1):
        for t in range(N):
            for par in (0, 1):
                r = mat * 16 + 2 * t + par
                total = csum[r : r + 1, :]
                for e in range(1, N):
                    q = mat * 16 + 2 * minus(t, e) + par
                    total = total + tsum_in[e - 1, q : q + 1, :]
                c = (2 * t + par) * B
                col_inv[mat, :, c : c + B] = jnp.broadcast_to(half / total, (8, B))

    def weight_tile(i, carry):
        r = pl.multiple_of(i // 8 * 512, 512)
        c = pl.multiple_of(lax.rem(i, 8) * 256, 256)
        for part in range(2):
            cc = c + part * B
            a = es[pl.ds(r, 512), pl.ds(cc, B)] * (row_inv[0, pl.ds(r, 512), :] + col_inv[0, 0:1, pl.ds(cc, B)])
            b = et[pl.ds(r, 512), pl.ds(cc, B)] * (row_inv[1, pl.ds(r, 512), :] + col_inv[1, 0:1, pl.ds(cc, B)])
            w[pl.ds(r, 512), pl.ds(cc, B)] = (a - b).astype(jnp.bfloat16)
        return carry

    lax.fori_loop(0, 16, weight_tile, 0)

    def grad_copy(side, slot):
        back = minus(0, slot) - 1
        src = di.at[pl.ds(slot * B, B), :] if side == 0 else dt_out.at[slot]
        return pltpu.make_async_remote_copy(
            src_ref=src,
            dst_ref=(di_in, dt_in)[side].at[back],
            send_sem=grad_send.at[side, slot - 1],
            recv_sem=grad_recv.at[side, back],
            device_id=peers[side](*SLOTS[slot]),
            device_id_type=MESH,
        )

    def grad_from(side, slot):
        return pltpu.make_async_remote_copy(
            src_ref=di.at[pl.ds(slot * B, B), :] if side == 0 else dt_out.at[slot],
            dst_ref=(di_in, dt_in)[side].at[slot - 1],
            send_sem=grad_send.at[side, slot - 1],
            recv_sem=grad_recv.at[side, slot - 1],
            device_id=peers[side](*SLOTS[slot]),
            device_id_type=MESH,
        )

    def grad_sib(slot):
        return pltpu.make_async_remote_copy(
            src_ref=dt_other.at[slot], dst_ref=dt_sib.at[slot],
            send_sem=grad_sib_send.at[slot], recv_sem=grad_sib_recv.at[slot],
            device_id=sibling, device_id_type=MESH,
        )

    def text_terms(s):
        out = jnp.dot(ist[...], w[:, 2 * s * B : 2 * (s + 1) * B], preferred_element_type=jnp.float32)
        dt_keep[s] = out[:, 0:B]
        dt_other[s] = out[:, B : 2 * B].astype(jnp.bfloat16)
        grad_sib(s).start()

    def text_send(s):
        grad_sib(s).wait_recv()
        dt_out[s] = (dt_keep[s] + dt_sib[s].astype(jnp.float32)).astype(jnp.bfloat16)
        grad_copy(1, s).start()

    def image_terms(s):
        out = jnp.dot(w[s * B : (s + 2) * B, :], xs[...], preferred_element_type=jnp.float32)
        di[s * B : (s + 2) * B, :] = out.astype(jnp.bfloat16)
        if s == 0:
            own_di[...] = out[0:B, :]
        for t in (s + 1, s):
            if t:
                grad_copy(0, t).start()

    text_terms(7)
    text_terms(4)
    image_terms(6)
    text_send(7)
    text_send(4)
    text_terms(6)
    text_terms(5)
    image_terms(4)
    text_send(6)
    text_send(5)
    text_terms(3)
    text_terms(2)
    image_terms(2)
    text_send(3)
    text_send(2)
    text_terms(1)
    text_terms(0)
    image_terms(0)
    text_send(1)
    grad_sib(0).wait_recv()

    def finish(raw, total):
        norm, inverse = unit_rows(raw)
        return inverse * (total - norm * jnp.sum(norm * total, axis=1, keepdims=True))

    total = own_di[...]
    for slot in range(1, N):
        grad_from(0, slot).wait_recv()
        total = total + di_in[slot - 1].astype(jnp.float32)
    gi_ref[...] = finish(si_ref[...], total)
    total = dt_keep[0] + dt_sib[0].astype(jnp.float32)
    for slot in range(1, N):
        grad_from(1, slot).wait_recv()
        total = total + dt_in[slot - 1].astype(jnp.float32)
    gt_ref[...] = finish(st_ref[...], total.T)

    for side in (0, 1):
        for i in range(N_HOPS):
            hop(side, i).wait_send()
        for slot in range(1, N):
            sum_copy(side, slot).wait_send()
            grad_copy(side, slot).wait_send()
    for slot in range(N):
        to_sibling(slot, "T").wait_send()
        to_sibling(slot, "S").wait_send()
        grad_sib(slot).wait_send()
    tsum_to_sib.wait_send()


def per_device(teacher_image, student_image, teacher_text, student_text):
    f32, bf16 = jnp.float32, jnp.bfloat16
    vmem = pl.BlockSpec(memory_space=pltpu.VMEM)
    dma = pltpu.SemaphoreType.DMA
    return pl.pallas_call(
        kernel,
        out_shape=(jax.ShapeDtypeStruct((B, 512), f32), jax.ShapeDtypeStruct((B, 512), f32)),
        in_specs=[vmem] * 4,
        out_specs=(vmem, vmem),
        scratch_shapes=[
            pltpu.VMEM((N * B, 1024), bf16),
            pltpu.VMEM((N * B, 512), bf16),
            pltpu.VMEM((2 * N * B, 1024), bf16),
            pltpu.VMEM((2 * N * B, 512), bf16),
            pltpu.VMEM((N * B, 2 * N * B), f32),
            pltpu.VMEM((N * B, 2 * N * B), f32),
            pltpu.VMEM((N * B, 2 * N * B), bf16),
            pltpu.VMEM((512, N * B), bf16),
            pltpu.VMEM((2, N * B, B), f32),
            pltpu.VMEM((2, 8, 2 * N * B), f32),
            pltpu.VMEM((2, N * B, B), f32),
            pltpu.VMEM((2, 8, 2 * N * B), f32),
            pltpu.VMEM((16, B), f32),
            pltpu.VMEM((7, 16, B), f32),
            pltpu.VMEM((32, B), f32),
            pltpu.VMEM((32, B), f32),
            pltpu.VMEM((32, B), f32),
            pltpu.VMEM((7, 32, B), f32),
            pltpu.VMEM((N * B, 512), bf16),
            pltpu.VMEM((7, B, 512), bf16),
            pltpu.VMEM((B, 512), f32),
            pltpu.VMEM((N, 512, B), f32),
            pltpu.VMEM((N, 512, B), bf16),
            pltpu.VMEM((N, 512, B), bf16),
            pltpu.VMEM((N, 512, B), bf16),
            pltpu.VMEM((7, 512, B), bf16),
            dma((2, N_HOPS)),
            dma((2, N_HOPS)),
            dma((2, N)),
            dma((2, N)),
            dma((15,)),
            dma((15,)),
            dma((2, 7)),
            dma((2, 7)),
            dma((N,)),
            dma((N,)),
        ],
        compiler_params=pltpu.CompilerParams(
            collective_id=0, has_side_effects=True, vmem_limit_bytes=60 << 20
        ),
        cost_estimate=pl.CostEstimate(flops=10_737_418_240, bytes_accessed=1 << 20, transcendentals=1 << 22),
    )(teacher_image, student_image, teacher_text, student_text)


def solution(mesh):
    spec = P(("grp", "row", "col"), None)
    return jax.shard_map(
        per_device, mesh=mesh, in_specs=(spec,) * 4, out_specs=(spec, spec), check_vma=False
    )
```

```python
import jax
import jax.numpy as jnp
from jax import lax
from jax.experimental import pallas as pl
from jax.experimental.pallas import tpu as pltpu
from jax.sharding import PartitionSpec as P

EPS = 1e-06
LOGIT_SCALE = 14.285714285714286
LOG2E = 1.4426950408889634
MESH = pl.DeviceIdType.MESH
B = 128
F32, BF16 = jnp.float32, jnp.bfloat16

SLOTS = [(0, 0), (0, 1), (1, 0), (3, 0), (2, 0), (1, 1), (3, 1), (2, 1)]
N = len(SLOTS)
ORDER = [2, 3, 4, 0, 1, 6, 5, 7]
POS = [ORDER.index(s) for s in range(N)]


def slot_of(step, side):
    return SLOTS.index((step % 4, side % 2))


def minus(a, b):
    return slot_of(SLOTS[a][0] - SLOTS[b][0], SLOTS[a][1] - SLOTS[b][1])


PLUS, MINUS, PAIR, ACROSS = (1, 0), (3, 0), (0, 1), (2, 0)
HOPS = [
    (0, 1, PAIR, "S"),
    (0, 3, PLUS, "T0"),
    (0, 2, MINUS, "T0"),
    (0, 1, PAIR, "T0"),
    (0, 3, PLUS, "T1"),
    (0, 2, MINUS, "T1"),
    (0, 3, PLUS, "S"),
    (0, 2, MINUS, "S"),
    (3, 6, PAIR, "T0"),
    (3, 4, PLUS, "T0"),
    (2, 5, PAIR, "T1"),
    (2, 4, MINUS, "T1"),
    (0, 1, PAIR, "T1"),
    (3, 6, PAIR, "T1"),
    (2, 5, PAIR, "T0"),
    (1, 6, PLUS, "S"),
    (1, 5, MINUS, "S"),
    (3, 4, PLUS, "S0"),
    (2, 4, MINUS, "S1"),
    (6, 7, PLUS, "T0"),
    (5, 7, MINUS, "T1"),
    (6, 7, PLUS, "S0"),
    (5, 7, MINUS, "S1"),
]
PIECE_ROWS = {"T0": (0, 64), "T1": (64, 64), "S": (0, 128), "S0": (0, 64), "S1": (64, 64)}
N_HOPS = len(HOPS)
GRAD_TO = {7: PAIR, 5: PLUS, 6: MINUS, 2: PLUS, 3: MINUS, 4: ACROSS, 1: PAIR}
SINKS = {4: (7,), 1: (5, 6), 0: (2, 3, 4, 1)}


def dot_nt(a, b):
    return lax.dot_general(a, b, (((1,), (1,)), ((), ())), preferred_element_type=F32)


def unit_rows(raw):
    values = raw.astype(F32)
    inverse = lax.rsqrt(jnp.sum(values * values, axis=1, keepdims=True) + EPS)
    return values * inverse, inverse


def kernel(
    ti_hbm, si_hbm, tt_hbm, st_hbm, gi_ref, gt_ref,
    ti_ref, si_ref, tt_ref, st_ref,
    it, is_, xt, xs, es, et, w, ist,
    row_acc, col_acc, row_inv, col_inv,
    isum, isum_in, tsum, tsum_sib, csum, tsum_in,
    di_keep, di_out, di_in, dt_keep, dt_other, dt_sib, dt_out, dt_in,
    in_sems, hop_send, hop_recv, sib_send, sib_recv, sum_send, sum_recv,
    grad_send, grad_recv, grad_sib_send, grad_sib_recv,
):
    grp, row, col = lax.axis_index("grp"), lax.axis_index("row"), lax.axis_index("col")
    x_hi, z = col // 4, lax.rem(col, 4)
    y, core = row // 2, lax.rem(row, 2)

    def image_peer(step, side):
        to_grp = 1 - grp if side else grp
        return (to_grp, lax.rem(y + step, 4) * 2 + core, col)

    def text_peer(step, side):
        to_grp = 1 - grp if side else grp
        to_hi = 1 - x_hi if side else x_hi
        return (to_grp, row, to_hi * 4 + lax.rem(z + step, 4))

    peers = (image_peer, text_peer)
    sibling = (grp, y * 2 + 1 - core, col)
    started = []

    def go(copy):
        copy.start()
        started.append(copy)

    def remote(src, dst, send, recv, device):
        return pltpu.make_async_remote_copy(
            src_ref=src, dst_ref=dst, send_sem=send, recv_sem=recv, device_id=device, device_id_type=MESH
        )

    barrier = pltpu.get_barrier_semaphore()
    for peer in peers:
        for to in (PAIR, PLUS, MINUS):
            pl.semaphore_signal(barrier, inc=1, device_id=peer(*to), device_id_type=MESH)
    pl.semaphore_signal(barrier, inc=1, device_id=sibling, device_id_type=MESH)

    loads = [
        pltpu.make_async_copy(src, dst, in_sems.at[i])
        for i, (src, dst) in enumerate(((si_hbm, si_ref), (st_hbm, st_ref), (ti_hbm, ti_ref), (tt_hbm, tt_ref)))
    ]
    for load in loads:
        load.start()
    i0, t0 = POS[0] * B, 2 * POS[0] * B
    for load, raw, out, at in zip(loads, (si_ref, st_ref, ti_ref, tt_ref), (is_, xs, it, xt), (i0, t0, i0, t0)):
        load.wait()
        out[at : at + B, :] = unit_rows(raw[...])[0].astype(BF16)

    arrays = ((it, is_, 1), (xt, xs, 2))

    def piece_ref(side, slot, piece):
        teach, stud, stride = arrays[side]
        first, rows = PIECE_ROWS[piece]
        ref = teach if piece[0] == "T" else stud
        return ref.at[pl.ds(POS[slot] * stride * B + first, rows), :]

    def hop(side, i):
        src, dst, to, piece = HOPS[i]
        return remote(
            piece_ref(side, src, piece), piece_ref(side, dst, piece),
            hop_send.at[side, i], hop_recv.at[side, i], peers[side](*to),
        )

    def index(dst, piece):
        return next(i for i, h in enumerate(HOPS) if h[1] == dst and h[3] == piece)

    def send(*names):
        for dst, piece in names:
            for side in (0, 1):
                go(hop(side, index(dst, piece)))

    def arrived(*names):
        for dst, piece in names:
            for side in (0, 1):
                hop(side, index(dst, piece)).wait_recv()

    def to_sibling(slot, kind):
        ref = xt if kind == "T" else xs
        k = 0 if kind == "T" else 1
        return remote(
            ref.at[pl.ds(2 * POS[slot] * B, B), :], ref.at[pl.ds((2 * POS[slot] + 1) * B, B), :],
            sib_send.at[k, slot], sib_recv.at[k, slot], sibling,
        )

    def share(kind, *slots):
        for slot in slots:
            go(to_sibling(slot, kind))

    def shared(kind, *slots):
        for slot in slots:
            to_sibling(slot, kind).wait_recv()

    def logits(mat, rows, cols):
        left, right, out = ((is_, xs, es), (it, xt, et))[mat]
        for c in range(cols[0] * 2 * B, cols[1] * 2 * B, 2 * B):
            r = rows[0] * B
            while r < rows[1] * B:
                n = min(512, rows[1] * B - r)
                e = jnp.exp2(dot_nt(left[r : r + n, :], right[c : c + 256, :]) * (LOGIT_SCALE * LOG2E))
                out[r : r + n, c : c + 256] = e
                row_acc[mat, r : r + n, :] += e[:, 0:128] + e[:, 128:256]
                col_acc[mat, :, c : c + 256] += jnp.sum(e.reshape(n // 8, 8, 256), axis=0)
                r += n

    pl.semaphore_wait(barrier, 7)

    send((1, "S"), (3, "T0"), (2, "T0"), (1, "T0"), (3, "T1"), (2, "T1"), (3, "S"), (2, "S"))
    share("T", 0)
    share("S", 0)

    row_acc[...] = jnp.zeros_like(row_acc)
    col_acc[...] = jnp.zeros_like(col_acc)

    arrived((3, "T0"))
    send((6, "T0"), (4, "T0"))
    arrived((1, "S"))
    share("S", 1)
    arrived((2, "T0"), (2, "T1"))
    send((5, "T1"), (4, "T1"), (1, "T1"))
    arrived((3, "T1"))
    send((6, "T1"), (5, "T0"), (6, "S"), (5, "S"))
    share("T", 2, 3)
    arrived((1, "T0"), (2, "S"), (3, "S"))
    send((4, "S0"), (4, "S1"))
    share("S", 2, 3)
    arrived((6, "T0"))
    send((7, "T0"))
    arrived((4, "T0"), (4, "T1"))
    share("T", 4)
    arrived((5, "T1"))
    send((7, "T1"))
    shared("T", 0, 2, 3, 4)
    logits(1, (0, 4), (0, 4))
    arrived((6, "S"), (5, "S"))
    send((7, "S0"), (7, "S1"))
    share("S", 6, 5)
    arrived((1, "T1"))
    share("T", 1)
    arrived((4, "S0"), (4, "S1"))
    share("S", 4)
    for s in (0, 1, 2, 3, 4, 5, 6):
        p = POS[s]
        ist[:, p * B : (p + 1) * B] = is_[p * B : (p + 1) * B, :].T
    shared("S", 0, 1, 2, 3, 4, 5, 6)
    logits(0, (0, 6), (0, 6))
    arrived((6, "T1"))
    share("T", 6)
    shared("T", 1, 6)
    logits(1, (4, 6), (0, 6))
    logits(1, (0, 4), (4, 6))
    arrived((7, "T0"), (7, "T1"), (5, "T0"))
    share("T", 7, 5)
    arrived((7, "S0"), (7, "S1"))
    share("S", 7)
    logits(1, (6, 8), (0, 6))
    logits(0, (6, 8), (0, 6))
    p = POS[7]
    ist[:, p * B : (p + 1) * B] = is_[p * B : (p + 1) * B, :].T
    shared("T", 7, 5)
    shared("S", 7)
    logits(1, (0, 8), (6, 8))
    logits(0, (0, 8), (6, 8))

    for mat in (0, 1):
        for b in range(2 * N):
            r = mat * 16 + b
            tsum[r : r + 1, :] = jnp.sum(col_acc[mat, :, b * B : (b + 1) * B], axis=0, keepdims=True)
    tsum_to_sib = remote(tsum, tsum_sib, sum_send.at[14], sum_recv.at[14], sibling)
    go(tsum_to_sib)
    for mat in (0, 1):
        for p in range(N):
            part = row_acc[mat, p * B : (p + 1) * B, :]
            isum[mat * N + p : mat * N + p + 1, :] = jnp.sum(part.T, axis=0, keepdims=True)

    def sum_copy(side, slot):
        back = minus(0, slot) - 1
        return remote(
            (isum, csum)[side], (isum_in, tsum_in)[side].at[back],
            sum_send.at[side * 7 + slot - 1], sum_recv.at[side * 7 + back], peers[side](*SLOTS[slot]),
        )

    def sum_from(side, slot):
        return remote(
            (isum, csum)[side], (isum_in, tsum_in)[side].at[slot - 1],
            sum_send.at[side * 7 + slot - 1], sum_recv.at[side * 7 + slot - 1], peers[side](*SLOTS[slot]),
        )

    for slot in range(N - 1, 0, -1):
        go(sum_copy(0, slot))
    tsum_to_sib.wait_recv()
    for mat in (0, 1):
        for p in range(N):
            r = mat * 16 + 2 * p
            csum[r : r + 1, :] = tsum[r : r + 1, :] + tsum_sib[r + 1 : r + 2, :]
            csum[r + 1 : r + 2, :] = tsum[r + 1 : r + 2, :] + tsum_sib[r : r + 1, :]
    for slot in range(N - 1, 0, -1):
        go(sum_copy(1, slot))

    half = 0.5 * LOGIT_SCALE
    for slot in range(1, N):
        sum_from(0, slot).wait_recv()
    for mat in (0, 1):
        for t in range(N):
            r = mat * N + POS[t]
            total = isum[r : r + 1, :]
            for e in range(1, N):
                q = mat * N + POS[minus(t, e)]
                total = total + isum_in[e - 1, q : q + 1, :]
            row_inv[mat, POS[t] * B : (POS[t] + 1) * B, :] = jnp.broadcast_to(half / total, (B, B)).T
    for slot in range(1, N):
        sum_from(1, slot).wait_recv()
    for mat in (0, 1):
        for t in range(N):
            for par in (0, 1):
                r = mat * 16 + 2 * POS[t] + par
                total = csum[r : r + 1, :]
                for e in range(1, N):
                    q = mat * 16 + 2 * POS[minus(t, e)] + par
                    total = total + tsum_in[e - 1, q : q + 1, :]
                c = (2 * POS[t] + par) * B
                col_inv[mat, :, c : c + B] = jnp.broadcast_to(half / total, (8, B))

    def weights(rows, cols):
        for r in range(rows[0] * B, rows[1] * B, 64):
            for c in range(cols[0] * 2 * B, cols[1] * 2 * B, B):
                terms = []
                for mat, e in ((0, es), (1, et)):
                    factor = row_inv[mat, r : r + 64, :].reshape(8, 8, B) + col_inv[mat, :, c : c + B][None]
                    terms.append(e[r : r + 64, c : c + B].reshape(8, 8, B) * factor)
                w[r : r + 64, c : c + B] = (terms[0] - terms[1]).reshape(64, B).astype(BF16)

    def grad_copy(side, slot):
        return remote(
            (di_out, dt_out)[side].at[slot], (di_in, dt_in)[side].at[slot],
            grad_send.at[side, slot], grad_recv.at[side, slot], peers[side](*GRAD_TO[slot]),
        )

    def grad_sib(slot):
        return remote(
            dt_other.at[slot], dt_sib.at[slot], grad_sib_send.at[slot], grad_sib_recv.at[slot], sibling
        )

    def text_terms(*slots):
        for slot in slots:
            c = 2 * POS[slot] * B
            out = jnp.dot(ist[...], w[:, c : c + 2 * B], preferred_element_type=F32)
            dt_keep[slot] = out[:, 0:B]
            dt_other[slot] = out[:, B : 2 * B].astype(BF16)
            go(grad_sib(slot))

    def total_of(side, slot):
        if side == 0:
            total = di_keep[slot]
        else:
            grad_sib(slot).wait_recv()
            total = dt_keep[slot] + dt_sib[slot].astype(F32)
        for source in SINKS.get(slot, ()):
            grad_copy(side, source).wait_recv()
            total = total + (di_in, dt_in)[side][source].astype(F32)
        return total

    def grad_send_from(side, *slots):
        for slot in slots:
            (di_out, dt_out)[side][slot] = total_of(side, slot).astype(BF16)
            go(grad_copy(side, slot))

    def image_terms(p0, p1):
        out = jnp.dot(w[p0 * B : p1 * B, :], xs[...], preferred_element_type=F32)
        for p in range(p0, p1):
            part = out[(p - p0) * B : (p - p0 + 1) * B, :]
            if ORDER[p] in SINKS:
                di_keep[ORDER[p]] = part
            else:
                di_out[ORDER[p]] = part.astype(BF16)
        for p in range(p1 - 1, p0 - 1, -1):
            if ORDER[p] not in SINKS:
                go(grad_copy(0, ORDER[p]))

    weights((0, 8), (5, 8))
    text_terms(7, 5, 6)
    weights((5, 8), (0, 5))
    image_terms(5, 8)
    grad_send_from(1, 7, 5, 6)
    weights((0, 5), (0, 5))
    text_terms(2, 3)
    image_terms(0, 2)
    grad_send_from(1, 2, 3)
    text_terms(4, 1, 0)
    image_terms(2, 5)
    grad_send_from(0, 4, 1)
    grad_send_from(1, 4, 1)

    def finish(raw, total):
        norm, inverse = unit_rows(raw)
        return inverse * (total - norm * jnp.sum(norm * total, axis=1, keepdims=True))

    gi_ref[...] = finish(si_ref[...], total_of(0, 0))
    gt_ref[...] = finish(st_ref[...], total_of(1, 0).T)

    for copy in started:
        copy.wait_send()


def per_device(teacher_image, student_image, teacher_text, student_text):
    vmem, anywhere = pl.BlockSpec(memory_space=pltpu.VMEM), pl.BlockSpec(memory_space=pl.ANY)
    dma = pltpu.SemaphoreType.DMA
    return pl.pallas_call(
        kernel,
        out_shape=(jax.ShapeDtypeStruct((B, 512), F32), jax.ShapeDtypeStruct((B, 512), F32)),
        in_specs=[anywhere] * 4,
        out_specs=(vmem, vmem),
        scratch_shapes=[
            pltpu.VMEM((B, 1024), BF16),
            pltpu.VMEM((B, 512), BF16),
            pltpu.VMEM((B, 1024), BF16),
            pltpu.VMEM((B, 512), BF16),
            pltpu.VMEM((N * B, 1024), BF16),
            pltpu.VMEM((N * B, 512), BF16),
            pltpu.VMEM((2 * N * B, 1024), BF16),
            pltpu.VMEM((2 * N * B, 512), BF16),
            pltpu.VMEM((N * B, 2 * N * B), F32),
            pltpu.VMEM((N * B, 2 * N * B), F32),
            pltpu.VMEM((N * B, 2 * N * B), BF16),
            pltpu.VMEM((512, N * B), BF16),
            pltpu.VMEM((2, N * B, B), F32),
            pltpu.VMEM((2, 8, 2 * N * B), F32),
            pltpu.VMEM((2, N * B, B), F32),
            pltpu.VMEM((2, 8, 2 * N * B), F32),
            pltpu.VMEM((16, B), F32),
            pltpu.VMEM((7, 16, B), F32),
            pltpu.VMEM((32, B), F32),
            pltpu.VMEM((32, B), F32),
            pltpu.VMEM((32, B), F32),
            pltpu.VMEM((7, 32, B), F32),
            pltpu.VMEM((N, B, 512), F32),
            pltpu.VMEM((N, B, 512), BF16),
            pltpu.VMEM((N, B, 512), BF16),
            pltpu.VMEM((N, 512, B), F32),
            pltpu.VMEM((N, 512, B), BF16),
            pltpu.VMEM((N, 512, B), BF16),
            pltpu.VMEM((N, 512, B), BF16),
            pltpu.VMEM((N, 512, B), BF16),
            dma((4,)),
            dma((2, N_HOPS)),
            dma((2, N_HOPS)),
            dma((2, N)),
            dma((2, N)),
            dma((15,)),
            dma((15,)),
            dma((2, N)),
            dma((2, N)),
            dma((N,)),
            dma((N,)),
        ],
        compiler_params=pltpu.CompilerParams(
            collective_id=0, has_side_effects=True, vmem_limit_bytes=60 << 20
        ),
        cost_estimate=pl.CostEstimate(flops=10_737_418_240, bytes_accessed=1 << 20, transcendentals=1 << 22),
    )(teacher_image, student_image, teacher_text, student_text)


def solution(mesh):
    spec = P(("grp", "row", "col"), None)
    return jax.shard_map(
        per_device, mesh=mesh, in_specs=(spec,) * 4, out_specs=(spec, spec), check_vma=False
    )
```

```python
import jax
import jax.numpy as jnp
from jax import lax
from jax.experimental import pallas as pl
from jax.experimental.pallas import tpu as pltpu
from jax.sharding import PartitionSpec as P

EPS = 1e-06
LOGIT_SCALE = 14.285714285714286
LOG2E = 1.4426950408889634
MESH = pl.DeviceIdType.MESH
B = 128
F32, BF16 = jnp.float32, jnp.bfloat16

SLOTS = [(0, 0), (0, 1), (1, 0), (3, 0), (2, 0), (1, 1), (3, 1), (2, 1)]
N = len(SLOTS)
ORDER = [0, 2, 3, 4, 5, 6, 1, 7]
POS = [ORDER.index(s) for s in range(N)]


def slot_of(step, side):
    return SLOTS.index((step % 4, side % 2))


def minus(a, b):
    return slot_of(SLOTS[a][0] - SLOTS[b][0], SLOTS[a][1] - SLOTS[b][1])


PLUS, MINUS, PAIR, ACROSS = (1, 0), (3, 0), (0, 1), (2, 0)
HOPS = [
    (0, 1, PAIR, "S"),
    (0, 3, PLUS, "T0"),
    (0, 2, MINUS, "T0"),
    (0, 1, PAIR, "T0"),
    (0, 3, PLUS, "T1"),
    (0, 2, MINUS, "T1"),
    (0, 3, PLUS, "S"),
    (0, 2, MINUS, "S"),
    (3, 6, PAIR, "T0"),
    (3, 4, PLUS, "T0"),
    (2, 5, PAIR, "T1"),
    (2, 4, MINUS, "T1"),
    (3, 6, PAIR, "T1"),
    (0, 1, PAIR, "T1"),
    (1, 5, MINUS, "T0"),
    (1, 5, MINUS, "S"),
    (3, 4, PLUS, "S"),
    (1, 6, PLUS, "S"),
    (6, 7, PLUS, "T0"),
    (5, 7, MINUS, "T1"),
    (4, 7, PAIR, "S"),
]
PIECE_ROWS = {"T0": (0, 64), "T1": (64, 64), "S": (0, 128)}
N_HOPS = len(HOPS)
GRAD_TO = {7: PAIR, 5: PLUS, 6: MINUS, 2: PLUS, 3: MINUS, 4: ACROSS, 1: PAIR}
SINKS = {4: (7,), 1: (5, 6), 0: (2, 3, 1, 4)}


def dot_nt(a, b):
    return lax.dot_general(a, b, (((1,), (1,)), ((), ())), preferred_element_type=F32)


def unit_rows(raw):
    values = raw.astype(F32)
    inverse = lax.rsqrt(jnp.sum(values * values, axis=1, keepdims=True) + EPS)
    return values * inverse, inverse


def kernel(
    ti_hbm, si_hbm, tt_hbm, st_hbm, gi_ref, gt_ref,
    ti_ref, si_ref, tt_ref, st_ref,
    it, is_, xt, xs, es, et, w, ist,
    row_acc, col_acc, row_inv, col_inv,
    isum, isum_in, tsum, tsum_sib, csum, tsum_in,
    di_keep, di_out, di_in, dt_keep, dt_other, dt_sib, dt_out, dt_in,
    in_sems, hop_send, hop_recv, sib_send, sib_recv, sum_send, sum_recv,
    grad_send, grad_recv, grad_sib_send, grad_sib_recv,
):
    grp, row, col = lax.axis_index("grp"), lax.axis_index("row"), lax.axis_index("col")
    x_hi, z = col // 4, lax.rem(col, 4)
    y, core = row // 2, lax.rem(row, 2)

    def image_peer(step, side):
        to_grp = 1 - grp if side else grp
        return (to_grp, lax.rem(y + step, 4) * 2 + core, col)

    def text_peer(step, side):
        to_grp = 1 - grp if side else grp
        to_hi = 1 - x_hi if side else x_hi
        return (to_grp, row, to_hi * 4 + lax.rem(z + step, 4))

    peers = (image_peer, text_peer)
    sibling = (grp, y * 2 + 1 - core, col)
    started = []

    def segment(work):
        pl.when(grp >= 0)(work)

    def go(copy):
        copy.start()
        started.append(copy)

    def remote(src, dst, send, recv, device):
        return pltpu.make_async_remote_copy(
            src_ref=src, dst_ref=dst, send_sem=send, recv_sem=recv, device_id=device, device_id_type=MESH
        )

    barrier = pltpu.get_barrier_semaphore()
    for peer in peers:
        for to in (PAIR, PLUS, MINUS):
            pl.semaphore_signal(barrier, inc=1, device_id=peer(*to), device_id_type=MESH)
    pl.semaphore_signal(barrier, inc=1, device_id=sibling, device_id_type=MESH)

    loads = [
        pltpu.make_async_copy(src, dst, in_sems.at[i])
        for i, (src, dst) in enumerate(((si_hbm, si_ref), (st_hbm, st_ref), (ti_hbm, ti_ref), (tt_hbm, tt_ref)))
    ]
    for load in loads:
        load.start()
    i0, t0 = POS[0] * B, 2 * POS[0] * B
    for load, raw, out, at in zip(loads, (si_ref, st_ref, ti_ref, tt_ref), (is_, xs, it, xt), (i0, t0, i0, t0)):
        load.wait()
        out[at : at + B, :] = unit_rows(raw[...])[0].astype(BF16)

    arrays = ((it, is_, 1), (xt, xs, 2))

    def piece_ref(side, slot, piece):
        teach, stud, stride = arrays[side]
        first, rows = PIECE_ROWS[piece]
        ref = teach if piece[0] == "T" else stud
        return ref.at[pl.ds(POS[slot] * stride * B + first, rows), :]

    def hop(side, i):
        src, dst, to, piece = HOPS[i]
        return remote(
            piece_ref(side, src, piece), piece_ref(side, dst, piece),
            hop_send.at[side, i], hop_recv.at[side, i], peers[side](*to),
        )

    def index(dst, piece):
        return next(i for i, h in enumerate(HOPS) if h[1] == dst and h[3] == piece)

    def send(*names):
        for dst, piece in names:
            for side in (0, 1):
                go(hop(side, index(dst, piece)))

    def arrived(*names):
        for dst, piece in names:
            for side in (0, 1):
                hop(side, index(dst, piece)).wait_recv()

    def to_sibling(slot, kind):
        ref = xt if kind == "T" else xs
        k = 0 if kind == "T" else 1
        return remote(
            ref.at[pl.ds(2 * POS[slot] * B, B), :], ref.at[pl.ds((2 * POS[slot] + 1) * B, B), :],
            sib_send.at[k, slot], sib_recv.at[k, slot], sibling,
        )

    def share(kind, *slots):
        for slot in slots:
            go(to_sibling(slot, kind))

    def shared(kind, *slots):
        for slot in slots:
            to_sibling(slot, kind).wait_recv()

    def logits(mat, rows, cols):
        left, right, out = ((is_, xs, es), (it, xt, et))[mat]
        for c in range(cols[0] * 2 * B, cols[1] * 2 * B, 2 * B):
            r = rows[0] * B
            while r < rows[1] * B:
                n = min(512, rows[1] * B - r)
                e = jnp.exp2(dot_nt(left[r : r + n, :], right[c : c + 256, :]) * (LOGIT_SCALE * LOG2E))
                out[r : r + n, c : c + 256] = e
                row_acc[mat, r : r + n, :] += e[:, 0:128] + e[:, 128:256]
                col_acc[mat, :, c : c + 256] += jnp.sum(e.reshape(n // 8, 8, 256), axis=0)
                r += n

    pl.semaphore_wait(barrier, 7)

    send((1, "S"), (3, "T0"), (2, "T0"), (1, "T0"), (3, "T1"), (2, "T1"), (3, "S"), (2, "S"))
    share("T", 0)
    share("S", 0)

    @segment
    def _():
        row_acc[...] = jnp.zeros_like(row_acc)
        col_acc[...] = jnp.zeros_like(col_acc)

    arrived((3, "T0"))
    send((6, "T0"), (4, "T0"))
    arrived((1, "S"))
    share("S", 1)
    arrived((2, "T0"), (2, "T1"))
    send((5, "T1"), (4, "T1"))
    arrived((3, "T1"))
    send((6, "T1"), (1, "T1"))
    arrived((1, "T0"))
    send((5, "T0"), (5, "S"))
    share("T", 2, 3)
    arrived((3, "S"))
    send((4, "S"), (6, "S"))
    arrived((2, "S"))
    share("S", 2, 3)
    arrived((6, "T0"))
    send((7, "T0"))
    shared("T", 0, 2, 3)

    @segment
    def _():
        logits(1, (0, 3), (0, 3))

    shared("S", 0, 1, 2, 3)

    @segment
    def _():
        logits(0, (0, 3), (0, 3))
        logits(0, (0, 3), (6, 7))

    arrived((4, "T0"), (4, "T1"))
    share("T", 4)
    arrived((5, "T1"))
    send((7, "T1"))
    arrived((4, "S"))
    send((7, "S"))
    share("S", 4)
    arrived((5, "T0"), (6, "T1"))
    share("T", 5, 6)
    shared("T", 4)

    @segment
    def _():
        logits(1, (0, 3), (3, 4))
        logits(1, (3, 6), (0, 4))

    shared("T", 5, 6)

    @segment
    def _():
        logits(1, (0, 6), (4, 6))

    arrived((5, "S"), (6, "S"))
    share("S", 5, 6)
    arrived((1, "T1"))
    share("T", 1)

    @segment
    def _():
        logits(0, (3, 6), (0, 3))
        logits(0, (3, 6), (6, 7))

    shared("S", 4, 5, 6)

    @segment
    def _():
        logits(0, (0, 6), (3, 6))

    shared("T", 1)

    @segment
    def _():
        logits(1, (0, 6), (6, 7))

    arrived((7, "T0"), (7, "T1"))
    share("T", 7)
    arrived((7, "S"))
    share("S", 7)

    @segment
    def _():
        logits(1, (6, 8), (0, 7))
        logits(0, (6, 8), (0, 7))

    shared("T", 7)
    shared("S", 7)

    @segment
    def _():
        logits(1, (0, 8), (7, 8))
        logits(0, (0, 8), (7, 8))

    @segment
    def _():
        for mat in (0, 1):
            for b in range(2 * N):
                r = mat * 16 + b
                tsum[r : r + 1, :] = jnp.sum(col_acc[mat, :, b * B : (b + 1) * B], axis=0, keepdims=True)

    tsum_to_sib = remote(tsum, tsum_sib, sum_send.at[14], sum_recv.at[14], sibling)
    go(tsum_to_sib)

    @segment
    def _():
        for mat in (0, 1):
            for p in range(N):
                part = row_acc[mat, p * B : (p + 1) * B, :]
                isum[mat * N + p : mat * N + p + 1, :] = jnp.sum(part.T, axis=0, keepdims=True)

    def sum_copy(side, slot):
        back = minus(0, slot) - 1
        return remote(
            (isum, csum)[side], (isum_in, tsum_in)[side].at[back],
            sum_send.at[side * 7 + slot - 1], sum_recv.at[side * 7 + back], peers[side](*SLOTS[slot]),
        )

    def sum_from(side, slot):
        return remote(
            (isum, csum)[side], (isum_in, tsum_in)[side].at[slot - 1],
            sum_send.at[side * 7 + slot - 1], sum_recv.at[side * 7 + slot - 1], peers[side](*SLOTS[slot]),
        )

    for slot in range(N - 1, 0, -1):
        go(sum_copy(0, slot))
    tsum_to_sib.wait_recv()
    for mat in (0, 1):
        for p in range(N):
            r = mat * 16 + 2 * p
            csum[r : r + 1, :] = tsum[r : r + 1, :] + tsum_sib[r + 1 : r + 2, :]
            csum[r + 1 : r + 2, :] = tsum[r + 1 : r + 2, :] + tsum_sib[r : r + 1, :]
    for slot in range(N - 1, 0, -1):
        go(sum_copy(1, slot))

    @segment
    def _():
        for p in range(N):
            ist[:, p * B : (p + 1) * B] = is_[p * B : (p + 1) * B, :].T

    half = 0.5 * LOGIT_SCALE
    for slot in range(1, N):
        sum_from(0, slot).wait_recv()
    for mat in (0, 1):
        for t in range(N):
            r = mat * N + POS[t]
            total = isum[r : r + 1, :]
            for e in range(1, N):
                q = mat * N + POS[minus(t, e)]
                total = total + isum_in[e - 1, q : q + 1, :]
            row_inv[mat, POS[t] * B : (POS[t] + 1) * B, :] = jnp.broadcast_to(half / total, (B, B)).T
    for slot in range(1, N):
        sum_from(1, slot).wait_recv()
    for mat in (0, 1):
        for t in range(N):
            for par in (0, 1):
                r = mat * 16 + 2 * POS[t] + par
                total = csum[r : r + 1, :]
                for e in range(1, N):
                    q = mat * 16 + 2 * POS[minus(t, e)] + par
                    total = total + tsum_in[e - 1, q : q + 1, :]
                c = (2 * POS[t] + par) * B
                col_inv[mat, :, c : c + B] = jnp.broadcast_to(half / total, (8, B))

    def weights(rows, cols):
        for r in range(rows[0] * B, rows[1] * B, 64):
            for c in range(cols[0] * 2 * B, cols[1] * 2 * B, B):
                terms = []
                for mat, e in ((0, es), (1, et)):
                    factor = row_inv[mat, r : r + 64, :].reshape(8, 8, B) + col_inv[mat, :, c : c + B][None]
                    terms.append(e[r : r + 64, c : c + B].reshape(8, 8, B) * factor)
                w[r : r + 64, c : c + B] = (terms[0] - terms[1]).reshape(64, B).astype(BF16)

    def grad_copy(side, slot):
        return remote(
            (di_out, dt_out)[side].at[slot], (di_in, dt_in)[side].at[slot],
            grad_send.at[side, slot], grad_recv.at[side, slot], peers[side](*GRAD_TO[slot]),
        )

    def grad_sib(slot):
        return remote(
            dt_other.at[slot], dt_sib.at[slot], grad_sib_send.at[slot], grad_sib_recv.at[slot], sibling
        )

    def text_terms(*slots):
        for slot in slots:
            c = 2 * POS[slot] * B
            out = jnp.dot(ist[...], w[:, c : c + 2 * B], preferred_element_type=F32)
            dt_keep[slot] = out[:, 0:B]
            dt_other[slot] = out[:, B : 2 * B].astype(BF16)

    def text_share(*slots):
        for slot in slots:
            go(grad_sib(slot))

    def total_of(side, slot):
        if side == 0:
            total = di_keep[slot]
        else:
            grad_sib(slot).wait_recv()
            total = dt_keep[slot] + dt_sib[slot].astype(F32)
        for source in SINKS.get(slot, ()):
            grad_copy(side, source).wait_recv()
            total = total + (di_in, dt_in)[side][source].astype(F32)
        return total

    def grad_send_from(side, *slots):
        for slot in slots:
            (di_out, dt_out)[side][slot] = total_of(side, slot).astype(BF16)
            go(grad_copy(side, slot))

    def image_terms(p0, p1):
        out = jnp.dot(w[p0 * B : p1 * B, :], xs[...], preferred_element_type=F32)
        for p in range(p0, p1):
            part = out[(p - p0) * B : (p - p0 + 1) * B, :]
            if ORDER[p] in SINKS:
                di_keep[ORDER[p]] = part
            else:
                di_out[ORDER[p]] = part.astype(BF16)

    def image_send(*slots):
        for slot in slots:
            go(grad_copy(0, slot))

    @segment
    def _():
        weights((0, 8), (7, 8))
        text_terms(7)

    text_share(7)

    @segment
    def _():
        weights((0, 8), (4, 6))
        text_terms(5, 6)

    text_share(5, 6)

    @segment
    def _():
        weights((6, 8), (0, 4))
        weights((6, 8), (6, 7))
        image_terms(6, 8)

    image_send(7)
    grad_send_from(1, 7)

    @segment
    def _():
        weights((4, 6), (0, 4))
        weights((4, 6), (6, 7))
        image_terms(4, 6)

    image_send(5, 6)
    grad_send_from(1, 5, 6)

    @segment
    def _():
        weights((0, 4), (0, 4))
        text_terms(2, 3)

    text_share(2, 3)

    @segment
    def _():
        weights((0, 4), (6, 7))
        image_terms(0, 4)

    image_send(2, 3)
    grad_send_from(1, 2, 3)

    @segment
    def _():
        text_terms(4, 1, 0)

    text_share(4, 1, 0)
    grad_send_from(0, 4)
    grad_send_from(1, 4)
    grad_send_from(0, 1)
    grad_send_from(1, 1)

    def finish(raw, total):
        norm, inverse = unit_rows(raw)
        return inverse * (total - norm * jnp.sum(norm * total, axis=1, keepdims=True))

    gi_ref[...] = finish(si_ref[...], total_of(0, 0))
    gt_ref[...] = finish(st_ref[...], total_of(1, 0).T)

    for copy in started:
        copy.wait_send()


def per_device(teacher_image, student_image, teacher_text, student_text):
    vmem, anywhere = pl.BlockSpec(memory_space=pltpu.VMEM), pl.BlockSpec(memory_space=pl.ANY)
    dma = pltpu.SemaphoreType.DMA
    return pl.pallas_call(
        kernel,
        out_shape=(jax.ShapeDtypeStruct((B, 512), F32), jax.ShapeDtypeStruct((B, 512), F32)),
        in_specs=[anywhere] * 4,
        out_specs=(vmem, vmem),
        scratch_shapes=[
            pltpu.VMEM((B, 1024), BF16),
            pltpu.VMEM((B, 512), BF16),
            pltpu.VMEM((B, 1024), BF16),
            pltpu.VMEM((B, 512), BF16),
            pltpu.VMEM((N * B, 1024), BF16),
            pltpu.VMEM((N * B, 512), BF16),
            pltpu.VMEM((2 * N * B, 1024), BF16),
            pltpu.VMEM((2 * N * B, 512), BF16),
            pltpu.VMEM((N * B, 2 * N * B), F32),
            pltpu.VMEM((N * B, 2 * N * B), F32),
            pltpu.VMEM((N * B, 2 * N * B), BF16),
            pltpu.VMEM((512, N * B), BF16),
            pltpu.VMEM((2, N * B, B), F32),
            pltpu.VMEM((2, 8, 2 * N * B), F32),
            pltpu.VMEM((2, N * B, B), F32),
            pltpu.VMEM((2, 8, 2 * N * B), F32),
            pltpu.VMEM((16, B), F32),
            pltpu.VMEM((7, 16, B), F32),
            pltpu.VMEM((32, B), F32),
            pltpu.VMEM((32, B), F32),
            pltpu.VMEM((32, B), F32),
            pltpu.VMEM((7, 32, B), F32),
            pltpu.VMEM((N, B, 512), F32),
            pltpu.VMEM((N, B, 512), BF16),
            pltpu.VMEM((N, B, 512), BF16),
            pltpu.VMEM((N, 512, B), F32),
            pltpu.VMEM((N, 512, B), BF16),
            pltpu.VMEM((N, 512, B), BF16),
            pltpu.VMEM((N, 512, B), BF16),
            pltpu.VMEM((N, 512, B), BF16),
            dma((4,)),
            dma((2, N_HOPS)),
            dma((2, N_HOPS)),
            dma((2, N)),
            dma((2, N)),
            dma((15,)),
            dma((15,)),
            dma((2, N)),
            dma((2, N)),
            dma((N,)),
            dma((N,)),
        ],
        compiler_params=pltpu.CompilerParams(
            collective_id=0, has_side_effects=True, vmem_limit_bytes=60 << 20
        ),
        cost_estimate=pl.CostEstimate(flops=10_737_418_240, bytes_accessed=1 << 20, transcendentals=1 << 22),
    )(teacher_image, student_image, teacher_text, student_text)


def solution(mesh):
    spec = P(("grp", "row", "col"), None)
    return jax.shard_map(
        per_device, mesh=mesh, in_specs=(spec,) * 4, out_specs=(spec, spec), check_vma=False
    )
```

```python
import jax
import jax.numpy as jnp
from jax import lax
from jax.experimental import pallas as pl
from jax.experimental.pallas import tpu as pltpu
from jax.sharding import PartitionSpec as P

EPS = 1e-06
LOGIT_SCALE = 14.285714285714286
LOG2E = 1.4426950408889634
MESH = pl.DeviceIdType.MESH
B = 128
F32, BF16 = jnp.float32, jnp.bfloat16

SLOTS = [(0, 0), (0, 1), (1, 0), (3, 0), (2, 0), (1, 1), (3, 1), (2, 1)]
N = len(SLOTS)
ORDER = [0, 2, 3, 4, 1, 7, 5, 6]
POS = [ORDER.index(s) for s in range(N)]


def slot_of(step, side):
    return SLOTS.index((step % 4, side % 2))


def minus(a, b):
    return slot_of(SLOTS[a][0] - SLOTS[b][0], SLOTS[a][1] - SLOTS[b][1])


PLUS, MINUS, PAIR, ACROSS = (1, 0), (3, 0), (0, 1), (2, 0)
HOPS = [
    (0, 1, PAIR, "S"),
    (0, 3, PLUS, "T0"),
    (0, 2, MINUS, "T0"),
    (0, 1, PAIR, "T0"),
    (0, 3, PLUS, "T1"),
    (0, 2, MINUS, "T1"),
    (0, 3, PLUS, "S"),
    (0, 2, MINUS, "S"),
    (3, 6, PAIR, "T0"),
    (3, 4, PLUS, "T0"),
    (2, 5, PAIR, "T1"),
    (2, 4, MINUS, "T1"),
    (3, 6, PAIR, "T1"),
    (0, 1, PAIR, "T1"),
    (1, 5, MINUS, "T0"),
    (1, 5, MINUS, "S"),
    (3, 4, PLUS, "S"),
    (1, 6, PLUS, "S"),
    (6, 7, PLUS, "T0"),
    (5, 7, MINUS, "T1"),
    (4, 7, PAIR, "S"),
]
PIECE_ROWS = {"T0": (0, 64), "T1": (64, 64), "S": (0, 128)}
N_HOPS = len(HOPS)
GRAD_TO = {7: PAIR, 5: PLUS, 6: MINUS, 2: PLUS, 3: MINUS, 4: ACROSS, 1: PAIR}
SINKS = {4: (7,), 1: (5, 6), 0: (2, 3, 1, 4)}
HALVED = ()


def dot_nt(a, b):
    return lax.dot_general(a, b, (((1,), (1,)), ((), ())), preferred_element_type=F32)


def unit_rows(raw):
    values = raw.astype(F32)
    inverse = lax.rsqrt(jnp.sum(values * values, axis=1, keepdims=True) + EPS)
    return values * inverse, inverse


def kernel(
    ti_hbm, si_hbm, tt_hbm, st_hbm, gi_ref, gt_ref,
    ti_ref, si_ref, tt_ref, st_ref,
    it, is_, xt, xs, es, et, w, ist,
    row_acc, col_acc, row_inv, col_inv,
    isum, isum_in, tsum, tsum_sib, csum, tsum_in,
    di_keep, di_out, di_in, dt_keep, dt_other, dt_sib, dt_out, dt_in,
    in_sems, hop_send, hop_recv, sib_send, sib_recv, sum_send, sum_recv,
    grad_send, grad_recv, grad_sib_send, grad_sib_recv,
):
    grp, row, col = lax.axis_index("grp"), lax.axis_index("row"), lax.axis_index("col")
    x_hi, z = col // 4, lax.rem(col, 4)
    y, core = row // 2, lax.rem(row, 2)

    def image_peer(step, side):
        to_grp = 1 - grp if side else grp
        return (to_grp, lax.rem(y + step, 4) * 2 + core, col)

    def text_peer(step, side):
        to_grp = 1 - grp if side else grp
        to_hi = 1 - x_hi if side else x_hi
        return (to_grp, row, to_hi * 4 + lax.rem(z + step, 4))

    peers = (image_peer, text_peer)
    sibling = (grp, y * 2 + 1 - core, col)
    started = []

    def segment(work):
        pl.when(grp >= 0)(work)

    def go(copy):
        copy.start()
        started.append(copy)

    def remote(src, dst, send, recv, device):
        return pltpu.make_async_remote_copy(
            src_ref=src, dst_ref=dst, send_sem=send, recv_sem=recv, device_id=device, device_id_type=MESH
        )

    barrier = pltpu.get_barrier_semaphore()
    for peer in peers:
        for to in (PAIR, PLUS, MINUS):
            pl.semaphore_signal(barrier, inc=1, device_id=peer(*to), device_id_type=MESH)
    pl.semaphore_signal(barrier, inc=1, device_id=sibling, device_id_type=MESH)

    loads = [
        pltpu.make_async_copy(src, dst, in_sems.at[i])
        for i, (src, dst) in enumerate(((si_hbm, si_ref), (st_hbm, st_ref), (ti_hbm, ti_ref), (tt_hbm, tt_ref)))
    ]
    for load in loads:
        load.start()
    i0, t0 = POS[0] * B, 2 * POS[0] * B

    def normalize(raw, out, at, first, rows):
        out[at + first : at + first + rows, :] = unit_rows(raw[first : first + rows, :])[0].astype(BF16)

    arrays = ((it, is_, 1), (xt, xs, 2))

    def piece_ref(side, slot, piece):
        teach, stud, stride = arrays[side]
        first, rows = PIECE_ROWS[piece]
        ref = teach if piece[0] == "T" else stud
        return ref.at[pl.ds(POS[slot] * stride * B + first, rows), :]

    def hop(side, i):
        src, dst, to, piece = HOPS[i]
        return remote(
            piece_ref(side, src, piece), piece_ref(side, dst, piece),
            hop_send.at[side, i], hop_recv.at[side, i], peers[side](*to),
        )

    def index(dst, piece):
        return next(i for i, h in enumerate(HOPS) if h[1] == dst and h[3] == piece)

    def send(*names):
        for dst, piece in names:
            for side in (0, 1):
                go(hop(side, index(dst, piece)))

    def arrived(*names, sides=(0, 1)):
        for dst, piece in names:
            for side in sides:
                hop(side, index(dst, piece)).wait_recv()

    def to_sibling(slot, kind):
        ref = xt if kind == "T" else xs
        k = 0 if kind == "T" else 1
        return remote(
            ref.at[pl.ds(2 * POS[slot] * B, B), :], ref.at[pl.ds((2 * POS[slot] + 1) * B, B), :],
            sib_send.at[k, slot], sib_recv.at[k, slot], sibling,
        )

    def share(kind, *slots):
        for slot in slots:
            go(to_sibling(slot, kind))

    def shared(kind, *slots):
        for slot in slots:
            to_sibling(slot, kind).wait_recv()

    def logits(mat, rows, cols):
        left, right, out = ((is_, xs, es), (it, xt, et))[mat]
        for c in range(cols[0] * 2 * B, cols[1] * 2 * B, 2 * B):
            r = rows[0] * B
            while r < rows[1] * B:
                n = min(512, rows[1] * B - r)
                e = jnp.exp2(dot_nt(left[r : r + n, :], right[c : c + 256, :]) * (LOGIT_SCALE * LOG2E))
                out[r : r + n, c : c + 256] = e
                row_acc[mat, r : r + n, :] += e[:, 0:128] + e[:, 128:256]
                col_acc[mat, :, c : c + 256] += jnp.sum(e.reshape(n // 8, 8, 256), axis=0)
                r += n

    loads[0].wait()
    loads[1].wait()
    normalize(si_ref, is_, i0, 0, B)
    normalize(st_ref, xs, t0, 0, B)
    pl.semaphore_wait(barrier, 7)
    send((1, "S"))
    loads[2].wait()
    loads[3].wait()

    @segment
    def _():
        normalize(ti_ref, it, i0, 0, 64)
        normalize(tt_ref, xt, t0, 0, 64)

    send((3, "T0"), (2, "T0"), (1, "T0"))

    @segment
    def _():
        normalize(ti_ref, it, i0, 64, 64)
        normalize(tt_ref, xt, t0, 64, 64)

    send((3, "T1"), (2, "T1"), (3, "S"), (2, "S"))
    share("T", 0)
    share("S", 0)

    @segment
    def _():
        row_acc[...] = jnp.zeros_like(row_acc)
        col_acc[...] = jnp.zeros_like(col_acc)

    arrived((3, "T0"))
    send((6, "T0"), (4, "T0"))
    arrived((1, "S"))
    share("S", 1)
    arrived((2, "T0"), (2, "T1"))
    send((5, "T1"), (4, "T1"))
    arrived((3, "T1"))
    send((6, "T1"), (1, "T1"))
    arrived((1, "T0"))
    send((5, "T0"))
    share("T", 2, 3)
    arrived((3, "S"))
    send((4, "S"))
    arrived((2, "S"))
    share("S", 2, 3)
    arrived((6, "T0"))
    send((7, "T0"), (6, "S"))
    shared("T", 0, 2, 3)

    @segment
    def _():
        logits(1, (0, 3), (0, 3))

    arrived((4, "T0"), (4, "T1"))
    share("T", 4)
    arrived((5, "T1"))
    send((7, "T1"), (5, "S"))
    shared("S", 0, 1, 2, 3)

    @segment
    def _():
        logits(0, (0, 3), (0, 3))
        logits(0, (0, 3), (4, 5))

    shared("T", 4)

    @segment
    def _():
        logits(1, (0, 3), (3, 4))
        logits(1, (3, 4), (0, 4))

    arrived((4, "S"))
    send((7, "S"))
    share("S", 4)
    arrived((5, "T0"), (6, "T1"))
    share("T", 5, 6)

    @segment
    def _():
        logits(1, (6, 8), (0, 4))

    shared("T", 5, 6)

    @segment
    def _():
        logits(1, (0, 4), (6, 8))
        logits(1, (6, 8), (6, 8))

    for slot, pieces in ((1, ("T1",)), (7, ("T0", "T1"))):
        arrived(*((slot, piece) for piece in pieces), sides=(1,))
        share("T", slot)
    arrived((1, "T1"), (7, "T0"), (7, "T1"), sides=(0,))
    shared("S", 4)

    @segment
    def _():
        logits(0, (3, 5), (0, 5))
        logits(0, (0, 3), (3, 4))
        logits(1, (4, 6), (0, 4))
        logits(1, (4, 6), (6, 8))

    shared("T", 1, 7)

    @segment
    def _():
        logits(1, (0, 4), (4, 6))

    for slot in (5, 6, 7):
        arrived((slot, "S"), sides=(1,))
        share("S", slot)

    @segment
    def _():
        logits(1, (4, 8), (4, 6))

    arrived((5, "S"), (6, "S"), (7, "S"), sides=(0,))

    def sum_sib(mat):
        return remote(tsum.at[mat], tsum_sib.at[mat], sum_send.at[mat, 14], sum_recv.at[mat, 14], sibling)

    def sum_copy(mat, side, slot):
        back = minus(0, slot) - 1
        return remote(
            (isum, csum)[side].at[mat], (isum_in, tsum_in)[side].at[mat, back],
            sum_send.at[mat, side * 7 + slot - 1], sum_recv.at[mat, side * 7 + back], peers[side](*SLOTS[slot]),
        )

    def sum_from(mat, side, slot):
        return remote(
            (isum, csum)[side].at[mat], (isum_in, tsum_in)[side].at[mat, slot - 1],
            sum_send.at[mat, side * 7 + slot - 1], sum_recv.at[mat, side * 7 + slot - 1], peers[side](*SLOTS[slot]),
        )

    def sums_out(mat):
        @segment
        def _():
            for b in range(2 * N):
                tsum[mat, b : b + 1, :] = jnp.sum(col_acc[mat, :, b * B : (b + 1) * B], axis=0, keepdims=True)

        go(sum_sib(mat))

        @segment
        def _():
            for p in range(N):
                isum[mat, p : p + 1, :] = jnp.sum(row_acc[mat, p * B : (p + 1) * B, :].T, axis=0, keepdims=True)

        for slot in range(N - 1, 0, -1):
            go(sum_copy(mat, 0, slot))

    def text_sums_out(mat):
        sum_sib(mat).wait_recv()

        @segment
        def _():
            for p in range(N):
                r = 2 * p
                csum[mat, r : r + 1, :] = tsum[mat, r : r + 1, :] + tsum_sib[mat, r + 1 : r + 2, :]
                csum[mat, r + 1 : r + 2, :] = tsum[mat, r + 1 : r + 2, :] + tsum_sib[mat, r : r + 1, :]

        for slot in range(N - 1, 0, -1):
            go(sum_copy(mat, 1, slot))

    half = 0.5 * LOGIT_SCALE

    def sums_in(mat):
        for slot in range(1, N):
            sum_from(mat, 0, slot).wait_recv()

        @segment
        def _():
            for t in range(N):
                total = isum[mat, POS[t] : POS[t] + 1, :]
                for e in range(1, N):
                    q = POS[minus(t, e)]
                    total = total + isum_in[mat, e - 1, q : q + 1, :]
                row_inv[mat, POS[t] * B : (POS[t] + 1) * B, :] = jnp.broadcast_to(half / total, (B, B)).T

        for slot in range(1, N):
            sum_from(mat, 1, slot).wait_recv()

        @segment
        def _():
            for t in range(N):
                for par in (0, 1):
                    r = 2 * POS[t] + par
                    total = csum[mat, r : r + 1, :]
                    for e in range(1, N):
                        q = 2 * POS[minus(t, e)] + par
                        total = total + tsum_in[mat, e - 1, q : q + 1, :]
                    col_inv[mat, :, r * B : (r + 1) * B] = jnp.broadcast_to(half / total, (8, B))

    def weighted(mat, e, r, c):
        factor = row_inv[mat, r : r + 64, :].reshape(8, 8, B) + col_inv[mat, :, c : c + B][None]
        return e[r : r + 64, c : c + B].reshape(8, 8, B) * factor

    sums_out(1)

    @segment
    def _():
        logits(0, (5, 8), (0, 5))

    text_sums_out(1)
    shared("S", 5, 6, 7)

    @segment
    def _():
        logits(0, (0, 8), (5, 8))

    sums_out(0)

    @segment
    def _():
        for p in range(N):
            ist[:, p * B : (p + 1) * B] = is_[p * B : (p + 1) * B, :].T

    text_sums_out(0)
    sums_in(1)

    @segment
    def _():
        for r in range(0, N * B, 64):
            for c in range(0, 2 * N * B, B):
                et[r : r + 64, c : c + B] = weighted(1, et, r, c).reshape(64, B)

    sums_in(0)

    def weights(rows, cols):
        for r in range(rows[0] * B, rows[1] * B, 64):
            for c in range(cols[0] * 2 * B, cols[1] * 2 * B, B):
                term = weighted(0, es, r, c).reshape(64, B) - et[r : r + 64, c : c + B]
                w[r : r + 64, c : c + B] = term.astype(BF16)

    def halves(slot):
        return (0, 1) if slot in HALVED else (None,)

    def span(side, part):
        rows = (B, 512)[side]
        return (0, rows) if part is None else (part * rows // 2, rows // 2)

    def grad_copy(side, slot, part):
        first, rows = span(side, part)
        return remote(
            (di_out, dt_out)[side].at[slot, pl.ds(first, rows), :], (di_in, dt_in)[side].at[slot, pl.ds(first, rows), :],
            grad_send.at[side, slot, part or 0], grad_recv.at[side, slot, part or 0], peers[side](*GRAD_TO[slot]),
        )

    def grad_sib(slot):
        return remote(
            dt_other.at[slot], dt_sib.at[slot], grad_sib_send.at[slot], grad_sib_recv.at[slot], sibling
        )

    def text_terms(*slots):
        for slot in slots:
            c = 2 * POS[slot] * B
            out = jnp.dot(ist[...], w[:, c : c + 2 * B], preferred_element_type=F32)
            dt_keep[slot] = out[:, 0:B]
            dt_other[slot] = out[:, B : 2 * B].astype(BF16)

    def text_share(*slots):
        for slot in slots:
            go(grad_sib(slot))

    def total_of(side, slot, part=None):
        first, rows = span(side, part)
        at = pl.ds(first, rows)
        if side == 0:
            total = di_keep[slot, at, :]
        else:
            total = dt_keep[slot, at, :] + dt_sib[slot, at, :].astype(F32)
        for source in SINKS.get(slot, ()):
            for half_of in halves(source) if part is None else (part,):
                grad_copy(side, source, half_of).wait_recv()
            total = total + (di_in, dt_in)[side][source, at, :].astype(F32)
        return total

    def grad_sum_send(side, slot, part=None):
        first, rows = span(side, part)
        (di_out, dt_out)[side][slot, pl.ds(first, rows), :] = total_of(side, slot, part).astype(BF16)
        go(grad_copy(side, slot, part))

    def text_send(*slots):
        for slot in slots:
            grad_sib(slot).wait_recv()
            for part in halves(slot):
                grad_sum_send(1, slot, part)

    def image_terms(p0, p1):
        out = jnp.dot(w[p0 * B : p1 * B, :], xs[...], preferred_element_type=F32)
        for p in range(p0, p1):
            part = out[(p - p0) * B : (p - p0 + 1) * B, :]
            if ORDER[p] in SINKS:
                di_keep[ORDER[p]] = part
            else:
                di_out[ORDER[p]] = part.astype(BF16)

    def image_send(*slots):
        for slot in slots:
            for part in halves(slot):
                go(grad_copy(0, slot, part))

    @segment
    def _():
        weights((0, 8), (5, 8))
        text_terms(7, 5, 6)

    text_share(7, 5, 6)

    @segment
    def _():
        weights((5, 8), (0, 5))
        image_terms(5, 8)

    image_send(7, 5, 6)
    text_send(7, 5, 6)

    @segment
    def _():
        weights((0, 5), (0, 5))
        text_terms(2, 3)

    text_share(2, 3)

    @segment
    def _():
        image_terms(1, 3)

    image_send(2, 3)
    text_send(2, 3)

    @segment
    def _():
        text_terms(4, 1, 0)

    text_share(4, 1, 0)

    @segment
    def _():
        image_terms(3, 5)
        image_terms(0, 1)

    grad_sum_send(0, 4)
    text_send(4)
    grad_sum_send(0, 1)
    text_send(1)
    grad_sib(0).wait_recv()

    def finish(raw, total):
        norm, inverse = unit_rows(raw)
        return inverse * (total - norm * jnp.sum(norm * total, axis=1, keepdims=True))

    gi_ref[...] = finish(si_ref[...], total_of(0, 0))
    gt_ref[...] = finish(st_ref[...], total_of(1, 0).T)

    for copy in started:
        copy.wait_send()


def per_device(teacher_image, student_image, teacher_text, student_text):
    vmem, anywhere = pl.BlockSpec(memory_space=pltpu.VMEM), pl.BlockSpec(memory_space=pl.ANY)
    dma = pltpu.SemaphoreType.DMA
    return pl.pallas_call(
        kernel,
        out_shape=(pltpu.VMEM((B, 512), F32), pltpu.VMEM((B, 512), F32)),
        in_specs=[anywhere] * 4,
        out_specs=(vmem, vmem),
        scratch_shapes=[
            pltpu.VMEM((B, 1024), BF16),
            pltpu.VMEM((B, 512), BF16),
            pltpu.VMEM((B, 1024), BF16),
            pltpu.VMEM((B, 512), BF16),
            pltpu.VMEM((N * B, 1024), BF16),
            pltpu.VMEM((N * B, 512), BF16),
            pltpu.VMEM((2 * N * B, 1024), BF16),
            pltpu.VMEM((2 * N * B, 512), BF16),
            pltpu.VMEM((N * B, 2 * N * B), F32),
            pltpu.VMEM((N * B, 2 * N * B), F32),
            pltpu.VMEM((N * B, 2 * N * B), BF16),
            pltpu.VMEM((512, N * B), BF16),
            pltpu.VMEM((2, N * B, B), F32),
            pltpu.VMEM((2, 8, 2 * N * B), F32),
            pltpu.VMEM((2, N * B, B), F32),
            pltpu.VMEM((2, 8, 2 * N * B), F32),
            pltpu.VMEM((2, N, B), F32),
            pltpu.VMEM((2, 7, N, B), F32),
            pltpu.VMEM((2, 2 * N, B), F32),
            pltpu.VMEM((2, 2 * N, B), F32),
            pltpu.VMEM((2, 2 * N, B), F32),
            pltpu.VMEM((2, 7, 2 * N, B), F32),
            pltpu.VMEM((N, B, 512), F32),
            pltpu.VMEM((N, B, 512), BF16),
            pltpu.VMEM((N, B, 512), BF16),
            pltpu.VMEM((N, 512, B), F32),
            pltpu.VMEM((N, 512, B), BF16),
            pltpu.VMEM((N, 512, B), BF16),
            pltpu.VMEM((N, 512, B), BF16),
            pltpu.VMEM((N, 512, B), BF16),
            dma((4,)),
            dma((2, N_HOPS)),
            dma((2, N_HOPS)),
            dma((2, N)),
            dma((2, N)),
            dma((2, 15)),
            dma((2, 15)),
            dma((2, N, 2)),
            dma((2, N, 2)),
            dma((N,)),
            dma((N,)),
        ],
        compiler_params=pltpu.CompilerParams(
            collective_id=0, has_side_effects=True, vmem_limit_bytes=60 << 20
        ),
        cost_estimate=pl.CostEstimate(flops=10_737_418_240, bytes_accessed=1 << 20, transcendentals=1 << 22),
    )(teacher_image, student_image, teacher_text, student_text)


def solution(mesh):
    spec = P(("grp", "row", "col"), None)
    return jax.shard_map(
        per_device, mesh=mesh, in_specs=(spec,) * 4, out_specs=(spec, spec), check_vma=False
    )
```

```python
import jax
import jax.numpy as jnp
from jax import lax
from jax.experimental import pallas as pl
from jax.experimental.pallas import tpu as pltpu
from jax.sharding import PartitionSpec as P

EPS = 1e-06
LOGIT_SCALE = 14.285714285714286
LOG2E = 1.4426950408889634
MESH = pl.DeviceIdType.MESH
B = 128
F32, BF16 = jnp.float32, jnp.bfloat16

SLOTS = [(0, 0), (0, 1), (1, 0), (3, 0), (2, 0), (1, 1), (3, 1), (2, 1)]
N = len(SLOTS)
ORDER = [0, 2, 3, 4, 1, 7, 5, 6]
POS = [ORDER.index(s) for s in range(N)]


def slot_of(step, side):
    return SLOTS.index((step % 4, side % 2))


def minus(a, b):
    return slot_of(SLOTS[a][0] - SLOTS[b][0], SLOTS[a][1] - SLOTS[b][1])


PLUS, MINUS, PAIR, ACROSS = (1, 0), (3, 0), (0, 1), (2, 0)
HOPS = [
    (0, 1, PAIR, "S"),
    (0, 3, PLUS, "T0"),
    (0, 2, MINUS, "T0"),
    (0, 1, PAIR, "T0"),
    (0, 3, PLUS, "T1"),
    (0, 2, MINUS, "T1"),
    (0, 3, PLUS, "S"),
    (0, 2, MINUS, "S"),
    (3, 6, PAIR, "T0"),
    (3, 4, PLUS, "T0"),
    (2, 5, PAIR, "T1"),
    (2, 4, MINUS, "T1"),
    (3, 6, PAIR, "T1"),
    (0, 1, PAIR, "T1"),
    (1, 5, MINUS, "T0"),
    (1, 5, MINUS, "S"),
    (3, 4, PLUS, "S"),
    (1, 6, PLUS, "S"),
    (6, 7, PLUS, "T0"),
    (5, 7, MINUS, "T1"),
    (4, 7, PAIR, "S"),
]
PIECE_ROWS = {"T0": (0, 64), "T1": (64, 64), "S": (0, 128)}
N_HOPS = len(HOPS)
GRAD_TO = {7: PAIR, 5: PLUS, 6: MINUS, 2: PLUS, 3: MINUS, 4: ACROSS, 1: PAIR}
SINKS = {4: (7,), 1: (5, 6), 0: (2, 3, 1, 4)}
HALVED = ()


def dot_nt(a, b):
    return lax.dot_general(a, b, (((1,), (1,)), ((), ())), preferred_element_type=F32)


def unit_rows(raw):
    values = raw.astype(F32)
    inverse = lax.rsqrt(jnp.sum(values * values, axis=1, keepdims=True) + EPS)
    return values * inverse, inverse


def kernel(
    ti_hbm, si_hbm, tt_hbm, st_hbm, gi_ref, gt_ref,
    ti_ref, si_ref, tt_ref, st_ref,
    it, is_, xt, xs, es, et, w, ist,
    row_acc, col_acc, row_inv, col_inv,
    isum, isum_in, tsum, tsum_sib, csum, tsum_in,
    di_keep, di_out, di_in, dt_keep, dt_other, dt_sib, dt_out, dt_in,
    in_sems, hop_send, hop_recv, sib_send, sib_recv, sum_send, sum_recv,
    grad_send, grad_recv, grad_sib_send, grad_sib_recv,
):
    grp, row, col = lax.axis_index("grp"), lax.axis_index("row"), lax.axis_index("col")
    x_hi, z = col // 4, lax.rem(col, 4)
    y, core = row // 2, lax.rem(row, 2)

    def image_peer(step, side):
        to_grp = 1 - grp if side else grp
        return (to_grp, lax.rem(y + step, 4) * 2 + core, col)

    def text_peer(step, side):
        to_grp = 1 - grp if side else grp
        to_hi = 1 - x_hi if side else x_hi
        return (to_grp, row, to_hi * 4 + lax.rem(z + step, 4))

    peers = (image_peer, text_peer)
    sibling = (grp, y * 2 + 1 - core, col)
    started = []

    def segment(work):
        pl.when(grp >= 0)(work)

    def go(copy):
        copy.start()
        started.append(copy)

    def remote(src, dst, send, recv, device):
        return pltpu.make_async_remote_copy(
            src_ref=src, dst_ref=dst, send_sem=send, recv_sem=recv, device_id=device, device_id_type=MESH
        )

    barrier = pltpu.get_barrier_semaphore()
    for peer in peers:
        for to in (PAIR, PLUS, MINUS):
            pl.semaphore_signal(barrier, inc=1, device_id=peer(*to), device_id_type=MESH)
    pl.semaphore_signal(barrier, inc=1, device_id=sibling, device_id_type=MESH)

    loads = [
        pltpu.make_async_copy(src, dst, in_sems.at[i])
        for i, (src, dst) in enumerate(((si_hbm, si_ref), (st_hbm, st_ref), (ti_hbm, ti_ref), (tt_hbm, tt_ref)))
    ]
    for load in loads:
        load.start()
    i0, t0 = POS[0] * B, 2 * POS[0] * B

    def normalize(raw, out, at, first, rows):
        out[at + first : at + first + rows, :] = unit_rows(raw[first : first + rows, :])[0].astype(BF16)

    arrays = ((it, is_, 1), (xt, xs, 2))

    def piece_ref(side, slot, piece):
        teach, stud, stride = arrays[side]
        first, rows = PIECE_ROWS[piece]
        ref = teach if piece[0] == "T" else stud
        return ref.at[pl.ds(POS[slot] * stride * B + first, rows), :]

    def hop(side, i):
        src, dst, to, piece = HOPS[i]
        return remote(
            piece_ref(side, src, piece), piece_ref(side, dst, piece),
            hop_send.at[side, i], hop_recv.at[side, i], peers[side](*to),
        )

    def index(dst, piece):
        return next(i for i, h in enumerate(HOPS) if h[1] == dst and h[3] == piece)

    def send(*names):
        for dst, piece in names:
            for side in (0, 1):
                go(hop(side, index(dst, piece)))

    def arrived(*names, sides=(0, 1)):
        for dst, piece in names:
            for side in sides:
                hop(side, index(dst, piece)).wait_recv()

    def to_sibling(slot, kind):
        ref = xt if kind == "T" else xs
        k = 0 if kind == "T" else 1
        return remote(
            ref.at[pl.ds(2 * POS[slot] * B, B), :], ref.at[pl.ds((2 * POS[slot] + 1) * B, B), :],
            sib_send.at[k, slot], sib_recv.at[k, slot], sibling,
        )

    def share(kind, *slots):
        for slot in slots:
            go(to_sibling(slot, kind))

    def shared(kind, *slots):
        for slot in slots:
            to_sibling(slot, kind).wait_recv()

    def logits(mat, rows, cols):
        left, right, out = ((is_, xs, es), (it, xt, et))[mat]
        for c in range(cols[0] * 2 * B, cols[1] * 2 * B, 2 * B):
            r = rows[0] * B
            while r < rows[1] * B:
                n = min(512, rows[1] * B - r)
                e = jnp.exp2(dot_nt(left[r : r + n, :], right[c : c + 256, :]) * (LOGIT_SCALE * LOG2E))
                out[r : r + n, c : c + 256] = e
                row_acc[mat, r : r + n, :] += e[:, 0:128] + e[:, 128:256]
                col_acc[mat, :, c : c + 256] += jnp.sum(e.reshape(n // 8, 8, 256), axis=0)
                r += n

    loads[0].wait()
    loads[1].wait()
    normalize(si_ref, is_, i0, 0, B)
    normalize(st_ref, xs, t0, 0, B)
    loads[2].wait()
    loads[3].wait()
    normalize(ti_ref, it, i0, 0, B)
    normalize(tt_ref, xt, t0, 0, B)
    pl.semaphore_wait(barrier, 7)
    send((1, "S"), (3, "T0"), (2, "T0"), (1, "T0"), (3, "T1"), (2, "T1"), (3, "S"), (2, "S"))
    share("T", 0)
    share("S", 0)

    @segment
    def _():
        row_acc[...] = jnp.zeros_like(row_acc)
        col_acc[...] = jnp.zeros_like(col_acc)

    arrived((3, "T0"))
    send((6, "T0"), (4, "T0"))
    arrived((1, "S"))
    share("S", 1)
    arrived((2, "T0"), (2, "T1"))
    send((5, "T1"), (4, "T1"))
    arrived((3, "T1"))
    send((6, "T1"), (1, "T1"))
    arrived((1, "T0"))
    send((5, "T0"))
    share("T", 2, 3)
    arrived((3, "S"))
    send((4, "S"))
    arrived((2, "S"))
    share("S", 2, 3)
    arrived((6, "T0"))
    send((7, "T0"), (6, "S"))
    shared("T", 0, 2, 3)

    @segment
    def _():
        logits(1, (0, 3), (0, 3))

    arrived((4, "T0"), (4, "T1"))
    share("T", 4)
    arrived((5, "T1"))
    send((7, "T1"), (5, "S"))
    shared("S", 0, 1, 2, 3)

    @segment
    def _():
        logits(0, (0, 3), (0, 3))
        logits(0, (0, 3), (4, 5))

    shared("T", 4)

    @segment
    def _():
        logits(1, (0, 3), (3, 4))
        logits(1, (3, 4), (0, 4))

    arrived((4, "S"))
    send((7, "S"))
    share("S", 4)
    arrived((5, "T0"), (6, "T1"))
    share("T", 5, 6)

    @segment
    def _():
        logits(1, (6, 8), (0, 4))

    shared("T", 5, 6)

    @segment
    def _():
        logits(1, (0, 4), (6, 8))
        logits(1, (6, 8), (6, 8))

    for slot, pieces in ((1, ("T1",)), (7, ("T0", "T1"))):
        arrived(*((slot, piece) for piece in pieces), sides=(1,))
        share("T", slot)
    arrived((1, "T1"), (7, "T0"), (7, "T1"), sides=(0,))
    shared("S", 4)

    @segment
    def _():
        logits(0, (3, 5), (0, 5))
        logits(0, (0, 3), (3, 4))
        logits(1, (4, 6), (0, 4))
        logits(1, (4, 6), (6, 8))

    shared("T", 1, 7)

    @segment
    def _():
        logits(1, (0, 4), (4, 6))

    for slot in (5, 6, 7):
        arrived((slot, "S"), sides=(1,))
        share("S", slot)

    @segment
    def _():
        logits(1, (4, 8), (4, 6))

    arrived((5, "S"), (6, "S"), (7, "S"), sides=(0,))

    def sum_sib(mat):
        return remote(tsum.at[mat], tsum_sib.at[mat], sum_send.at[mat, 14], sum_recv.at[mat, 14], sibling)

    def sum_copy(mat, side, slot):
        back = minus(0, slot) - 1
        return remote(
            (isum, csum)[side].at[mat], (isum_in, tsum_in)[side].at[mat, back],
            sum_send.at[mat, side * 7 + slot - 1], sum_recv.at[mat, side * 7 + back], peers[side](*SLOTS[slot]),
        )

    def sum_from(mat, side, slot):
        return remote(
            (isum, csum)[side].at[mat], (isum_in, tsum_in)[side].at[mat, slot - 1],
            sum_send.at[mat, side * 7 + slot - 1], sum_recv.at[mat, side * 7 + slot - 1], peers[side](*SLOTS[slot]),
        )

    def sums_out(mat):
        @segment
        def _():
            for b in range(2 * N):
                tsum[mat, b : b + 1, :] = jnp.sum(col_acc[mat, :, b * B : (b + 1) * B], axis=0, keepdims=True)

        go(sum_sib(mat))

        @segment
        def _():
            for p in range(N):
                isum[mat, p : p + 1, :] = jnp.sum(row_acc[mat, p * B : (p + 1) * B, :].T, axis=0, keepdims=True)

        for slot in range(N - 1, 0, -1):
            go(sum_copy(mat, 0, slot))

    def text_sums_out(mat):
        sum_sib(mat).wait_recv()

        @segment
        def _():
            for p in range(N):
                r = 2 * p
                csum[mat, r : r + 1, :] = tsum[mat, r : r + 1, :] + tsum_sib[mat, r + 1 : r + 2, :]
                csum[mat, r + 1 : r + 2, :] = tsum[mat, r + 1 : r + 2, :] + tsum_sib[mat, r : r + 1, :]

        for slot in range(N - 1, 0, -1):
            go(sum_copy(mat, 1, slot))

    half = 0.5 * LOGIT_SCALE

    def sums_in(mat):
        for slot in range(1, N):
            sum_from(mat, 0, slot).wait_recv()

        @segment
        def _():
            for t in range(N):
                total = isum[mat, POS[t] : POS[t] + 1, :]
                for e in range(1, N):
                    q = POS[minus(t, e)]
                    total = total + isum_in[mat, e - 1, q : q + 1, :]
                row_inv[mat, POS[t] * B : (POS[t] + 1) * B, :] = jnp.broadcast_to(half / total, (B, B)).T

        for slot in range(1, N):
            sum_from(mat, 1, slot).wait_recv()

        @segment
        def _():
            for t in range(N):
                for par in (0, 1):
                    r = 2 * POS[t] + par
                    total = csum[mat, r : r + 1, :]
                    for e in range(1, N):
                        q = 2 * POS[minus(t, e)] + par
                        total = total + tsum_in[mat, e - 1, q : q + 1, :]
                    col_inv[mat, :, r * B : (r + 1) * B] = jnp.broadcast_to(half / total, (8, B))

    def weighted(mat, e, r, c):
        factor = row_inv[mat, r : r + 64, :].reshape(8, 8, B) + col_inv[mat, :, c : c + B][None]
        return e[r : r + 64, c : c + B].reshape(8, 8, B) * factor

    sums_out(1)

    @segment
    def _():
        logits(0, (5, 8), (0, 5))

    text_sums_out(1)
    shared("S", 5, 6, 7)

    @segment
    def _():
        logits(0, (0, 8), (5, 8))

    sums_out(0)

    @segment
    def _():
        for p in range(N):
            ist[:, p * B : (p + 1) * B] = is_[p * B : (p + 1) * B, :].T

    text_sums_out(0)
    sums_in(1)

    @segment
    def _():
        for r in range(0, N * B, 64):
            for c in range(0, 2 * N * B, B):
                et[r : r + 64, c : c + B] = weighted(1, et, r, c).reshape(64, B)

    sums_in(0)

    def weights(rows, cols):
        for r in range(rows[0] * B, rows[1] * B, 64):
            for c in range(cols[0] * 2 * B, cols[1] * 2 * B, B):
                term = weighted(0, es, r, c).reshape(64, B) - et[r : r + 64, c : c + B]
                w[r : r + 64, c : c + B] = term.astype(BF16)

    def halves(slot):
        return (0, 1) if slot in HALVED else (None,)

    def span(side, part):
        rows = (B, 512)[side]
        return (0, rows) if part is None else (part * rows // 2, rows // 2)

    def grad_copy(side, slot, part):
        first, rows = span(side, part)
        return remote(
            (di_out, dt_out)[side].at[slot, pl.ds(first, rows), :], (di_in, dt_in)[side].at[slot, pl.ds(first, rows), :],
            grad_send.at[side, slot, part or 0], grad_recv.at[side, slot, part or 0], peers[side](*GRAD_TO[slot]),
        )

    def grad_sib(slot):
        return remote(
            dt_other.at[slot], dt_sib.at[slot], grad_sib_send.at[slot], grad_sib_recv.at[slot], sibling
        )

    def text_terms(*slots):
        for slot in slots:
            c = 2 * POS[slot] * B
            out = jnp.dot(ist[...], w[:, c : c + 2 * B], preferred_element_type=F32)
            dt_keep[slot] = out[:, 0:B]
            dt_other[slot] = out[:, B : 2 * B].astype(BF16)

    def text_share(*slots):
        for slot in slots:
            go(grad_sib(slot))

    def total_of(side, slot, part=None):
        first, rows = span(side, part)
        at = pl.ds(first, rows)
        if side == 0:
            total = di_keep[slot, at, :]
        else:
            total = dt_keep[slot, at, :] + dt_sib[slot, at, :].astype(F32)
        for source in SINKS.get(slot, ()):
            for half_of in halves(source) if part is None else (part,):
                grad_copy(side, source, half_of).wait_recv()
            total = total + (di_in, dt_in)[side][source, at, :].astype(F32)
        return total

    def grad_sum_send(side, slot, part=None):
        first, rows = span(side, part)
        (di_out, dt_out)[side][slot, pl.ds(first, rows), :] = total_of(side, slot, part).astype(BF16)
        go(grad_copy(side, slot, part))

    def text_send(*slots):
        for slot in slots:
            grad_sib(slot).wait_recv()
            for part in halves(slot):
                grad_sum_send(1, slot, part)

    def image_terms(p0, p1):
        out = jnp.dot(w[p0 * B : p1 * B, :], xs[...], preferred_element_type=F32)
        for p in range(p0, p1):
            part = out[(p - p0) * B : (p - p0 + 1) * B, :]
            if ORDER[p] in SINKS:
                di_keep[ORDER[p]] = part
            else:
                di_out[ORDER[p]] = part.astype(BF16)

    def image_send(*slots):
        for slot in slots:
            for part in halves(slot):
                go(grad_copy(0, slot, part))

    @segment
    def _():
        weights((0, 8), (5, 8))
        text_terms(7, 5, 6)

    text_share(7, 5, 6)

    @segment
    def _():
        weights((5, 8), (0, 5))
        image_terms(5, 8)

    image_send(7, 5, 6)
    text_send(7, 5, 6)

    @segment
    def _():
        weights((0, 5), (0, 5))
        text_terms(2, 3)

    text_share(2, 3)

    @segment
    def _():
        image_terms(1, 3)

    image_send(2, 3)
    text_send(2, 3)

    @segment
    def _():
        text_terms(4, 1, 0)

    text_share(4, 1, 0)

    @segment
    def _():
        image_terms(3, 5)
        image_terms(0, 1)

    grad_sum_send(0, 4)
    text_send(4)
    grad_sum_send(0, 1)
    text_send(1)
    grad_sib(0).wait_recv()

    gi_ref[...] = total_of(0, 0)
    gt_ref[...] = total_of(1, 0).T

    for copy in started:
        copy.wait_send()


def finish_kernel(si_ref, st_ref, di_ref, dt_ref, gi_ref, gt_ref):
    for raw, total, out in ((si_ref, di_ref, gi_ref), (st_ref, dt_ref, gt_ref)):
        norm, inverse = unit_rows(raw[...])
        direction = total[...]
        out[...] = inverse * (direction - norm * jnp.sum(norm * direction, axis=1, keepdims=True))


def per_device(teacher_image, student_image, teacher_text, student_text):
    vmem, anywhere = pl.BlockSpec(memory_space=pltpu.VMEM), pl.BlockSpec(memory_space=pl.ANY)
    dma = pltpu.SemaphoreType.DMA
    directions = pl.pallas_call(
        kernel,
        out_shape=(pltpu.VMEM((B, 512), F32), pltpu.VMEM((B, 512), F32)),
        in_specs=[anywhere] * 4,
        out_specs=(vmem, vmem),
        scratch_shapes=[
            pltpu.VMEM((B, 1024), BF16),
            pltpu.VMEM((B, 512), BF16),
            pltpu.VMEM((B, 1024), BF16),
            pltpu.VMEM((B, 512), BF16),
            pltpu.VMEM((N * B, 1024), BF16),
            pltpu.VMEM((N * B, 512), BF16),
            pltpu.VMEM((2 * N * B, 1024), BF16),
            pltpu.VMEM((2 * N * B, 512), BF16),
            pltpu.VMEM((N * B, 2 * N * B), F32),
            pltpu.VMEM((N * B, 2 * N * B), F32),
            pltpu.VMEM((N * B, 2 * N * B), BF16),
            pltpu.VMEM((512, N * B), BF16),
            pltpu.VMEM((2, N * B, B), F32),
            pltpu.VMEM((2, 8, 2 * N * B), F32),
            pltpu.VMEM((2, N * B, B), F32),
            pltpu.VMEM((2, 8, 2 * N * B), F32),
            pltpu.VMEM((2, N, B), F32),
            pltpu.VMEM((2, 7, N, B), F32),
            pltpu.VMEM((2, 2 * N, B), F32),
            pltpu.VMEM((2, 2 * N, B), F32),
            pltpu.VMEM((2, 2 * N, B), F32),
            pltpu.VMEM((2, 7, 2 * N, B), F32),
            pltpu.VMEM((N, B, 512), F32),
            pltpu.VMEM((N, B, 512), BF16),
            pltpu.VMEM((N, B, 512), BF16),
            pltpu.VMEM((N, 512, B), F32),
            pltpu.VMEM((N, 512, B), BF16),
            pltpu.VMEM((N, 512, B), BF16),
            pltpu.VMEM((N, 512, B), BF16),
            pltpu.VMEM((N, 512, B), BF16),
            dma((4,)),
            dma((2, N_HOPS)),
            dma((2, N_HOPS)),
            dma((2, N)),
            dma((2, N)),
            dma((2, 15)),
            dma((2, 15)),
            dma((2, N, 2)),
            dma((2, N, 2)),
            dma((N,)),
            dma((N,)),
        ],
        compiler_params=pltpu.CompilerParams(
            collective_id=0, has_side_effects=True, vmem_limit_bytes=60 << 20
        ),
        cost_estimate=pl.CostEstimate(flops=10_737_418_240, bytes_accessed=1 << 20, transcendentals=1 << 22),
    )(teacher_image, student_image, teacher_text, student_text)
    out = jax.ShapeDtypeStruct((B, 512), F32)
    return pl.pallas_call(
        finish_kernel,
        out_shape=(out, out),
        in_specs=[vmem] * 4,
        out_specs=(vmem, vmem),
        compiler_params=pltpu.CompilerParams(vmem_limit_bytes=4 << 20),
    )(student_image, student_text, *directions)


def solution(mesh):
    spec = P(("grp", "row", "col"), None)
    return jax.shard_map(
        per_device, mesh=mesh, in_specs=(spec,) * 4, out_specs=(spec, spec), check_vma=False
    )
```

```python
import jax
import jax.numpy as jnp
from jax import lax
from jax.experimental import pallas as pl
from jax.experimental.pallas import tpu as pltpu
from jax.sharding import PartitionSpec as P

EPS = 1e-06
LOGIT_SCALE = 14.285714285714286
LOG2E = 1.4426950408889634
MESH = pl.DeviceIdType.MESH
B = 128
F32, BF16 = jnp.float32, jnp.bfloat16

SLOTS = [(0, 0), (0, 1), (1, 0), (3, 0), (2, 0), (1, 1), (3, 1), (2, 1)]
N = len(SLOTS)
ORDER = [0, 2, 3, 4, 1, 7, 5, 6]
POS = [ORDER.index(s) for s in range(N)]


def slot_of(step, side):
    return SLOTS.index((step % 4, side % 2))


def minus(a, b):
    return slot_of(SLOTS[a][0] - SLOTS[b][0], SLOTS[a][1] - SLOTS[b][1])


PLUS, MINUS, PAIR, ACROSS = (1, 0), (3, 0), (0, 1), (2, 0)
HOPS = [
    (0, 1, PAIR, "S"),
    (0, 3, PLUS, "T0"),
    (0, 2, MINUS, "T0"),
    (0, 1, PAIR, "T0"),
    (0, 3, PLUS, "T1"),
    (0, 2, MINUS, "T1"),
    (0, 3, PLUS, "S"),
    (0, 2, MINUS, "S"),
    (3, 6, PAIR, "T0"),
    (3, 4, PLUS, "T0"),
    (2, 5, PAIR, "T1"),
    (2, 4, MINUS, "T1"),
    (3, 6, PAIR, "T1"),
    (0, 1, PAIR, "T1"),
    (1, 5, MINUS, "T0"),
    (1, 5, MINUS, "S"),
    (3, 4, PLUS, "S"),
    (1, 6, PLUS, "S"),
    (6, 7, PLUS, "T0"),
    (5, 7, MINUS, "T1"),
    (4, 7, PAIR, "S"),
]
PIECE_ROWS = {"T0": (0, 64), "T1": (64, 64), "S": (0, 128)}
N_HOPS = len(HOPS)
GRAD_TO = {7: PAIR, 5: PLUS, 6: MINUS, 2: PLUS, 3: MINUS, 4: ACROSS, 1: PAIR}
SINKS = {4: (7,), 1: (5, 6), 0: (2, 3, 1, 4)}
HALVED = ()


def dot_nt(a, b):
    return lax.dot_general(a, b, (((1,), (1,)), ((), ())), preferred_element_type=F32)


def unit_rows(raw):
    values = raw.astype(F32)
    inverse = lax.rsqrt(jnp.sum(values * values, axis=1, keepdims=True) + EPS)
    return values * inverse, inverse


def kernel(
    ti_hbm, si_hbm, tt_hbm, st_hbm, gi_ref, gt_ref,
    ti_ref, si_ref, tt_ref, st_ref,
    it, is_, xt, xs, es, et, w, ist,
    row_acc, col_acc, row_inv, col_inv,
    isum, isum_in, tsum, tsum_sib, csum, tsum_in,
    di_keep, di_out, di_in, dt_keep, dt_other, dt_sib, dt_out, dt_in,
    in_sems, hop_send, hop_recv, sib_send, sib_recv, sum_send, sum_recv,
    grad_send, grad_recv, grad_sib_send, grad_sib_recv,
):
    grp, row, col = lax.axis_index("grp"), lax.axis_index("row"), lax.axis_index("col")
    x_hi, z = col // 4, lax.rem(col, 4)
    y, core = row // 2, lax.rem(row, 2)

    def image_peer(step, side):
        to_grp = 1 - grp if side else grp
        return (to_grp, lax.rem(y + step, 4) * 2 + core, col)

    def text_peer(step, side):
        to_grp = 1 - grp if side else grp
        to_hi = 1 - x_hi if side else x_hi
        return (to_grp, row, to_hi * 4 + lax.rem(z + step, 4))

    peers = (image_peer, text_peer)
    sibling = (grp, y * 2 + 1 - core, col)
    started = []

    def segment(work):
        pl.when(grp >= 0)(work)

    def go(copy):
        copy.start()
        started.append(copy)

    def drain(count):
        for copy in started[:count]:
            copy.wait_send()
        del started[:count]

    def remote(src, dst, send, recv, device):
        return pltpu.make_async_remote_copy(
            src_ref=src, dst_ref=dst, send_sem=send, recv_sem=recv, device_id=device, device_id_type=MESH
        )

    barrier = pltpu.get_barrier_semaphore()
    for peer in peers:
        for to in (PAIR, PLUS, MINUS):
            pl.semaphore_signal(barrier, inc=1, device_id=peer(*to), device_id_type=MESH)
    pl.semaphore_signal(barrier, inc=1, device_id=sibling, device_id_type=MESH)

    loads = [
        pltpu.make_async_copy(src, dst, in_sems.at[i])
        for i, (src, dst) in enumerate(((si_hbm, si_ref), (st_hbm, st_ref), (ti_hbm, ti_ref), (tt_hbm, tt_ref)))
    ]
    for load in loads:
        load.start()
    i0, t0 = POS[0] * B, 2 * POS[0] * B

    def normalize(raw, out, at, first, rows):
        out[at + first : at + first + rows, :] = unit_rows(raw[first : first + rows, :])[0].astype(BF16)

    arrays = ((it, is_, 1), (xt, xs, 2))

    def piece_ref(side, slot, piece):
        teach, stud, stride = arrays[side]
        first, rows = PIECE_ROWS[piece]
        ref = teach if piece[0] == "T" else stud
        return ref.at[pl.ds(POS[slot] * stride * B + first, rows), :]

    def hop(side, i):
        src, dst, to, piece = HOPS[i]
        return remote(
            piece_ref(side, src, piece), piece_ref(side, dst, piece),
            hop_send.at[side, i], hop_recv.at[side, i], peers[side](*to),
        )

    def index(dst, piece):
        return next(i for i, h in enumerate(HOPS) if h[1] == dst and h[3] == piece)

    def send(*names):
        for dst, piece in names:
            for side in (0, 1):
                go(hop(side, index(dst, piece)))

    def arrived(*names, sides=(0, 1)):
        for dst, piece in names:
            for side in sides:
                hop(side, index(dst, piece)).wait_recv()

    def to_sibling(slot, kind):
        ref = xt if kind == "T" else xs
        k = 0 if kind == "T" else 1
        return remote(
            ref.at[pl.ds(2 * POS[slot] * B, B), :], ref.at[pl.ds((2 * POS[slot] + 1) * B, B), :],
            sib_send.at[k, slot], sib_recv.at[k, slot], sibling,
        )

    def share(kind, *slots):
        for slot in slots:
            go(to_sibling(slot, kind))

    def shared(kind, *slots):
        for slot in slots:
            to_sibling(slot, kind).wait_recv()

    def logits(mat, rows, cols):
        left, right, out = ((is_, xs, es), (it, xt, et))[mat]
        for c in range(cols[0] * 2 * B, cols[1] * 2 * B, 2 * B):
            r = rows[0] * B
            while r < rows[1] * B:
                n = min(512, rows[1] * B - r)
                e = jnp.exp2(dot_nt(left[r : r + n, :], right[c : c + 256, :]) * (LOGIT_SCALE * LOG2E))
                out[r : r + n, c : c + 256] = e
                row_acc[mat, r : r + n, :] += e[:, 0:128] + e[:, 128:256]
                col_acc[mat, :, c : c + 256] += jnp.sum(e.reshape(n // 8, 8, 256), axis=0)
                r += n

    loads[0].wait()
    loads[1].wait()
    normalize(si_ref, is_, i0, 0, B)
    normalize(st_ref, xs, t0, 0, B)
    loads[2].wait()
    loads[3].wait()
    normalize(ti_ref, it, i0, 0, B)
    normalize(tt_ref, xt, t0, 0, B)
    pl.semaphore_wait(barrier, 7)
    send((1, "S"), (3, "T0"), (2, "T0"), (1, "T0"), (3, "T1"), (2, "T1"), (3, "S"), (2, "S"))
    share("T", 0)
    share("S", 0)

    @segment
    def _():
        row_acc[...] = jnp.zeros_like(row_acc)
        col_acc[...] = jnp.zeros_like(col_acc)

    arrived((3, "T0"))
    send((6, "T0"), (4, "T0"))
    arrived((1, "S"))
    share("S", 1)
    arrived((2, "T0"), (2, "T1"))
    send((5, "T1"), (4, "T1"))
    arrived((3, "T1"))
    send((6, "T1"), (1, "T1"))
    arrived((1, "T0"))
    send((5, "T0"))
    share("T", 2, 3)
    arrived((3, "S"))
    send((4, "S"))
    arrived((2, "S"))
    share("S", 2, 3)
    arrived((6, "T0"))
    send((7, "T0"), (6, "S"))
    shared("T", 0, 2, 3)

    @segment
    def _():
        logits(1, (0, 3), (0, 3))

    arrived((4, "T0"), (4, "T1"))
    share("T", 4)
    arrived((5, "T1"))
    send((7, "T1"), (5, "S"))
    shared("S", 0, 1, 2, 3)

    @segment
    def _():
        logits(0, (0, 3), (0, 3))
        logits(0, (0, 3), (4, 5))

    shared("T", 4)

    @segment
    def _():
        logits(1, (0, 3), (3, 4))
        logits(1, (3, 4), (0, 4))

    arrived((4, "S"))
    send((7, "S"))
    share("S", 4)
    arrived((5, "T0"), (6, "T1"))
    share("T", 5, 6)

    @segment
    def _():
        logits(1, (6, 8), (0, 4))

    shared("T", 5, 6)

    @segment
    def _():
        logits(1, (0, 4), (6, 8))
        logits(1, (6, 8), (6, 8))

    for slot, pieces in ((1, ("T1",)), (7, ("T0", "T1"))):
        arrived(*((slot, piece) for piece in pieces), sides=(1,))
        share("T", slot)
    arrived((1, "T1"), (7, "T0"), (7, "T1"), sides=(0,))
    shared("S", 4)

    @segment
    def _():
        logits(0, (3, 5), (0, 5))
        logits(0, (0, 3), (3, 4))
        logits(1, (4, 6), (0, 4))
        logits(1, (4, 6), (6, 8))

    shared("T", 1, 7)

    @segment
    def _():
        logits(1, (0, 4), (4, 6))

    for slot in (5, 6, 7):
        arrived((slot, "S"), sides=(1,))
        share("S", slot)

    @segment
    def _():
        logits(1, (4, 8), (4, 6))

    arrived((5, "S"), (6, "S"), (7, "S"), sides=(0,))

    def sum_sib(mat):
        return remote(tsum.at[mat], tsum_sib.at[mat], sum_send.at[mat, 14], sum_recv.at[mat, 14], sibling)

    def sum_copy(mat, side, slot):
        back = minus(0, slot) - 1
        return remote(
            (isum, csum)[side].at[mat], (isum_in, tsum_in)[side].at[mat, back],
            sum_send.at[mat, side * 7 + slot - 1], sum_recv.at[mat, side * 7 + back], peers[side](*SLOTS[slot]),
        )

    def sum_from(mat, side, slot):
        return remote(
            (isum, csum)[side].at[mat], (isum_in, tsum_in)[side].at[mat, slot - 1],
            sum_send.at[mat, side * 7 + slot - 1], sum_recv.at[mat, side * 7 + slot - 1], peers[side](*SLOTS[slot]),
        )

    def sums_out(mat):
        @segment
        def _():
            for b in range(2 * N):
                tsum[mat, b : b + 1, :] = jnp.sum(col_acc[mat, :, b * B : (b + 1) * B], axis=0, keepdims=True)

        go(sum_sib(mat))

        @segment
        def _():
            for p in range(N):
                isum[mat, p : p + 1, :] = jnp.sum(row_acc[mat, p * B : (p + 1) * B, :].T, axis=0, keepdims=True)

        for slot in range(N - 1, 0, -1):
            go(sum_copy(mat, 0, slot))

    def text_sums_out(mat):
        sum_sib(mat).wait_recv()

        @segment
        def _():
            for p in range(N):
                r = 2 * p
                csum[mat, r : r + 1, :] = tsum[mat, r : r + 1, :] + tsum_sib[mat, r + 1 : r + 2, :]
                csum[mat, r + 1 : r + 2, :] = tsum[mat, r + 1 : r + 2, :] + tsum_sib[mat, r : r + 1, :]

        for slot in range(N - 1, 0, -1):
            go(sum_copy(mat, 1, slot))

    half = 0.5 * LOGIT_SCALE

    def sums_in(mat):
        for slot in range(1, N):
            sum_from(mat, 0, slot).wait_recv()

        @segment
        def _():
            for t in range(N):
                total = isum[mat, POS[t] : POS[t] + 1, :]
                for e in range(1, N):
                    q = POS[minus(t, e)]
                    total = total + isum_in[mat, e - 1, q : q + 1, :]
                row_inv[mat, POS[t] * B : (POS[t] + 1) * B, :] = jnp.broadcast_to(half / total, (B, B)).T

        for slot in range(1, N):
            sum_from(mat, 1, slot).wait_recv()

        @segment
        def _():
            for t in range(N):
                for par in (0, 1):
                    r = 2 * POS[t] + par
                    total = csum[mat, r : r + 1, :]
                    for e in range(1, N):
                        q = 2 * POS[minus(t, e)] + par
                        total = total + tsum_in[mat, e - 1, q : q + 1, :]
                    col_inv[mat, :, r * B : (r + 1) * B] = jnp.broadcast_to(half / total, (8, B))

    def weighted(mat, e, r, c):
        factor = row_inv[mat, r : r + 64, :].reshape(8, 8, B) + col_inv[mat, :, c : c + B][None]
        return e[r : r + 64, c : c + B].reshape(8, 8, B) * factor

    sums_out(1)

    @segment
    def _():
        logits(0, (5, 8), (0, 5))

    text_sums_out(1)
    shared("S", 5, 6, 7)

    @segment
    def _():
        logits(0, (0, 8), (5, 8))

    gathered = len(started)
    sums_out(0)

    @segment
    def _():
        for p in range(N):
            ist[:, p * B : (p + 1) * B] = is_[p * B : (p + 1) * B, :].T

    text_sums_out(0)
    drain(gathered)
    sums_in(1)

    @segment
    def _():
        for r in range(0, N * B, 64):
            for c in range(0, 2 * N * B, B):
                et[r : r + 64, c : c + B] = weighted(1, et, r, c).reshape(64, B)

    sums_in(0)

    def weights(rows, cols):
        for r in range(rows[0] * B, rows[1] * B, 64):
            for c in range(cols[0] * 2 * B, cols[1] * 2 * B, B):
                term = weighted(0, es, r, c).reshape(64, B) - et[r : r + 64, c : c + B]
                w[r : r + 64, c : c + B] = term.astype(BF16)

    def halves(slot):
        return (0, 1) if slot in HALVED else (None,)

    def span(side, part):
        rows = (B, 512)[side]
        return (0, rows) if part is None else (part * rows // 2, rows // 2)

    def grad_copy(side, slot, part):
        first, rows = span(side, part)
        return remote(
            (di_out, dt_out)[side].at[slot, pl.ds(first, rows), :], (di_in, dt_in)[side].at[slot, pl.ds(first, rows), :],
            grad_send.at[side, slot, part or 0], grad_recv.at[side, slot, part or 0], peers[side](*GRAD_TO[slot]),
        )

    def grad_sib(slot):
        return remote(
            dt_other.at[slot], dt_sib.at[slot], grad_sib_send.at[slot], grad_sib_recv.at[slot], sibling
        )

    def text_terms(*slots):
        for slot in slots:
            c = 2 * POS[slot] * B
            out = jnp.dot(ist[...], w[:, c : c + 2 * B], preferred_element_type=F32)
            dt_keep[slot] = out[:, 0:B]
            dt_other[slot] = out[:, B : 2 * B].astype(BF16)

    def text_share(*slots):
        for slot in slots:
            go(grad_sib(slot))

    def total_of(side, slot, part=None):
        first, rows = span(side, part)
        at = pl.ds(first, rows)
        if side == 0:
            total = di_keep[slot, at, :]
        else:
            total = dt_keep[slot, at, :] + dt_sib[slot, at, :].astype(F32)
        for source in SINKS.get(slot, ()):
            for half_of in halves(source) if part is None else (part,):
                grad_copy(side, source, half_of).wait_recv()
            total = total + (di_in, dt_in)[side][source, at, :].astype(F32)
        return total

    def grad_sum_send(side, slot, part=None):
        first, rows = span(side, part)
        (di_out, dt_out)[side][slot, pl.ds(first, rows), :] = total_of(side, slot, part).astype(BF16)
        go(grad_copy(side, slot, part))

    def text_send(*slots):
        for slot in slots:
            grad_sib(slot).wait_recv()
            for part in halves(slot):
                grad_sum_send(1, slot, part)

    def image_terms(p0, p1):
        out = jnp.dot(w[p0 * B : p1 * B, :], xs[...], preferred_element_type=F32)
        for p in range(p0, p1):
            part = out[(p - p0) * B : (p - p0 + 1) * B, :]
            if ORDER[p] in SINKS:
                di_keep[ORDER[p]] = part
            else:
                di_out[ORDER[p]] = part.astype(BF16)

    def image_send(*slots):
        for slot in slots:
            for part in halves(slot):
                go(grad_copy(0, slot, part))

    summed = len(started)

    @segment
    def _():
        weights((0, 8), (6, 8))
        text_terms(5, 6)

    text_share(5, 6)

    @segment
    def _():
        weights((0, 8), (5, 6))
        text_terms(7)

    text_share(7)

    @segment
    def _():
        weights((5, 8), (0, 5))
        image_terms(5, 8)

    image_send(7, 5, 6)
    text_send(5, 6, 7)

    @segment
    def _():
        weights((0, 5), (1, 3))
        text_terms(2, 3)

    text_share(2, 3)

    @segment
    def _():
        weights((0, 5), (0, 1))
        weights((0, 5), (3, 5))
        image_terms(1, 3)

    image_send(2, 3)

    @segment
    def _():
        text_terms(4, 1)

    text_share(4, 1)
    text_send(2, 3)

    @segment
    def _():
        image_terms(3, 5)

    drain(summed)
    shared_terms = len(started)
    grad_sum_send(0, 4)
    text_send(4)
    grad_sum_send(0, 1)
    text_send(1)

    @segment
    def _():
        text_terms(0)

    text_share(0)

    @segment
    def _():
        image_terms(0, 1)

    grad_sib(0).wait_recv()
    drain(shared_terms)

    gi_ref[...] = total_of(0, 0)
    gt_ref[...] = total_of(1, 0).T

    drain(len(started))


def finish_kernel(si_ref, st_ref, di_ref, dt_ref, gi_ref, gt_ref):
    for raw, total, out in ((si_ref, di_ref, gi_ref), (st_ref, dt_ref, gt_ref)):
        norm, inverse = unit_rows(raw[...])
        direction = total[...]
        out[...] = inverse * (direction - norm * jnp.sum(norm * direction, axis=1, keepdims=True))


def per_device(teacher_image, student_image, teacher_text, student_text):
    vmem, anywhere = pl.BlockSpec(memory_space=pltpu.VMEM), pl.BlockSpec(memory_space=pl.ANY)
    dma = pltpu.SemaphoreType.DMA
    directions = pl.pallas_call(
        kernel,
        out_shape=(pltpu.VMEM((B, 512), F32), pltpu.VMEM((B, 512), F32)),
        in_specs=[anywhere] * 4,
        out_specs=(vmem, vmem),
        scratch_shapes=[
            pltpu.VMEM((B, 1024), BF16),
            pltpu.VMEM((B, 512), BF16),
            pltpu.VMEM((B, 1024), BF16),
            pltpu.VMEM((B, 512), BF16),
            pltpu.VMEM((N * B, 1024), BF16),
            pltpu.VMEM((N * B, 512), BF16),
            pltpu.VMEM((2 * N * B, 1024), BF16),
            pltpu.VMEM((2 * N * B, 512), BF16),
            pltpu.VMEM((N * B, 2 * N * B), F32),
            pltpu.VMEM((N * B, 2 * N * B), F32),
            pltpu.VMEM((N * B, 2 * N * B), BF16),
            pltpu.VMEM((512, N * B), BF16),
            pltpu.VMEM((2, N * B, B), F32),
            pltpu.VMEM((2, 8, 2 * N * B), F32),
            pltpu.VMEM((2, N * B, B), F32),
            pltpu.VMEM((2, 8, 2 * N * B), F32),
            pltpu.VMEM((2, N, B), F32),
            pltpu.VMEM((2, 7, N, B), F32),
            pltpu.VMEM((2, 2 * N, B), F32),
            pltpu.VMEM((2, 2 * N, B), F32),
            pltpu.VMEM((2, 2 * N, B), F32),
            pltpu.VMEM((2, 7, 2 * N, B), F32),
            pltpu.VMEM((N, B, 512), F32),
            pltpu.VMEM((N, B, 512), BF16),
            pltpu.VMEM((N, B, 512), BF16),
            pltpu.VMEM((N, 512, B), F32),
            pltpu.VMEM((N, 512, B), BF16),
            pltpu.VMEM((N, 512, B), BF16),
            pltpu.VMEM((N, 512, B), BF16),
            pltpu.VMEM((N, 512, B), BF16),
            dma((4,)),
            dma((2, N_HOPS)),
            dma((2, N_HOPS)),
            dma((2, N)),
            dma((2, N)),
            dma((2, 15)),
            dma((2, 15)),
            dma((2, N, 2)),
            dma((2, N, 2)),
            dma((N,)),
            dma((N,)),
        ],
        compiler_params=pltpu.CompilerParams(
            collective_id=0, has_side_effects=True, vmem_limit_bytes=60 << 20
        ),
        cost_estimate=pl.CostEstimate(flops=10_737_418_240, bytes_accessed=1 << 20, transcendentals=1 << 22),
    )(teacher_image, student_image, teacher_text, student_text)
    out = jax.ShapeDtypeStruct((B, 512), F32)
    return pl.pallas_call(
        finish_kernel,
        out_shape=(out, out),
        in_specs=[vmem] * 4,
        out_specs=(vmem, vmem),
        compiler_params=pltpu.CompilerParams(vmem_limit_bytes=4 << 20),
    )(student_image, student_text, *directions)


def solution(mesh):
    spec = P(("grp", "row", "col"), None)
    return jax.shard_map(
        per_device, mesh=mesh, in_specs=(spec,) * 4, out_specs=(spec, spec), check_vma=False
    )
```

```python
import jax
import jax.numpy as jnp
from jax import lax
from jax.experimental import pallas as pl
from jax.experimental.pallas import tpu as pltpu
from jax.sharding import PartitionSpec as P

EPS = 1e-06
LOGIT_SCALE = 14.285714285714286
LOG2E = 1.4426950408889634
MESH = pl.DeviceIdType.MESH
B = 128
F32, BF16 = jnp.float32, jnp.bfloat16

SLOTS = [(0, 0), (0, 1), (1, 0), (3, 0), (2, 0), (1, 1), (3, 1), (2, 1)]
N = len(SLOTS)
ORDER = [0, 2, 3, 4, 1, 7, 5, 6]
POS = [ORDER.index(s) for s in range(N)]


def slot_of(step, side):
    return SLOTS.index((step % 4, side % 2))


def minus(a, b):
    return slot_of(SLOTS[a][0] - SLOTS[b][0], SLOTS[a][1] - SLOTS[b][1])


PLUS, MINUS, PAIR, ACROSS = (1, 0), (3, 0), (0, 1), (2, 0)
HOPS = [
    (0, 1, PAIR, "S"),
    (0, 3, PLUS, "T0"),
    (0, 2, MINUS, "T0"),
    (0, 1, PAIR, "T0"),
    (0, 3, PLUS, "T1"),
    (0, 2, MINUS, "T1"),
    (0, 3, PLUS, "S"),
    (0, 2, MINUS, "S"),
    (3, 6, PAIR, "T0"),
    (3, 4, PLUS, "T0"),
    (2, 5, PAIR, "T1"),
    (2, 4, MINUS, "T1"),
    (3, 6, PAIR, "T1"),
    (0, 1, PAIR, "T1"),
    (1, 5, MINUS, "T0"),
    (1, 5, MINUS, "S"),
    (3, 4, PLUS, "S"),
    (1, 6, PLUS, "S"),
    (6, 7, PLUS, "T0"),
    (5, 7, MINUS, "T1"),
    (4, 7, PAIR, "S"),
]
PIECE_ROWS = {"T0": (0, 64), "T1": (64, 64), "S": (0, 128)}
N_HOPS = len(HOPS)
GRAD_TO = {7: PAIR, 5: PLUS, 6: MINUS, 2: PLUS, 3: MINUS, 4: ACROSS, 1: PAIR}
SINKS = {4: (7,), 1: (5, 6), 0: (2, 3, 1, 4)}
HALVED = ()


def dot_nt(a, b):
    return lax.dot_general(a, b, (((1,), (1,)), ((), ())), preferred_element_type=F32)


def unit_rows(raw):
    values = raw.astype(F32)
    inverse = lax.rsqrt(jnp.sum(values * values, axis=1, keepdims=True) + EPS)
    return values * inverse, inverse


def kernel(
    ti_hbm, si_hbm, tt_hbm, st_hbm, gi_ref, gt_ref,
    ti_ref, si_ref, tt_ref, st_ref,
    it, is_, xt, xs, es, et, w, ist,
    row_acc, col_acc, row_inv, col_inv,
    isum, isum_in, tsum, tsum_sib, csum, tsum_in,
    di_keep, di_out, di_in, dt_keep, dt_other, dt_sib, dt_out, dt_in,
    in_sems, hop_send, hop_recv, sib_send, sib_recv, sum_send, sum_recv,
    grad_send, grad_recv, grad_sib_send, grad_sib_recv,
):
    grp, row, col = lax.axis_index("grp"), lax.axis_index("row"), lax.axis_index("col")
    x_hi, z = col // 4, lax.rem(col, 4)
    y, core = row // 2, lax.rem(row, 2)

    def image_peer(step, side):
        to_grp = 1 - grp if side else grp
        return (to_grp, lax.rem(y + step, 4) * 2 + core, col)

    def text_peer(step, side):
        to_grp = 1 - grp if side else grp
        to_hi = 1 - x_hi if side else x_hi
        return (to_grp, row, to_hi * 4 + lax.rem(z + step, 4))

    peers = (image_peer, text_peer)
    sibling = (grp, y * 2 + 1 - core, col)
    started = []

    def segment(work):
        pl.when(grp >= 0)(work)

    def go(copy):
        copy.start()
        started.append(copy)

    def drain(count):
        for copy in started[:count]:
            copy.wait_send()
        del started[:count]

    def remote(src, dst, send, recv, device):
        return pltpu.make_async_remote_copy(
            src_ref=src, dst_ref=dst, send_sem=send, recv_sem=recv, device_id=device, device_id_type=MESH
        )

    barrier = pltpu.get_barrier_semaphore()
    for peer in peers:
        for to in (PAIR, PLUS, MINUS):
            pl.semaphore_signal(barrier, inc=1, device_id=peer(*to), device_id_type=MESH)
    pl.semaphore_signal(barrier, inc=1, device_id=sibling, device_id_type=MESH)

    loads = [
        pltpu.make_async_copy(src, dst, in_sems.at[i])
        for i, (src, dst) in enumerate(((si_hbm, si_ref), (st_hbm, st_ref), (ti_hbm, ti_ref), (tt_hbm, tt_ref)))
    ]
    for load in loads:
        load.start()
    i0, t0 = POS[0] * B, 2 * POS[0] * B

    def normalize(raw, out, at, first, rows):
        out[at + first : at + first + rows, :] = unit_rows(raw[first : first + rows, :])[0].astype(BF16)

    arrays = ((it, is_, 1), (xt, xs, 2))

    def piece_ref(side, slot, piece):
        teach, stud, stride = arrays[side]
        first, rows = PIECE_ROWS[piece]
        ref = teach if piece[0] == "T" else stud
        return ref.at[pl.ds(POS[slot] * stride * B + first, rows), :]

    def hop(side, i):
        src, dst, to, piece = HOPS[i]
        return remote(
            piece_ref(side, src, piece), piece_ref(side, dst, piece),
            hop_send.at[side, i], hop_recv.at[side, i], peers[side](*to),
        )

    def index(dst, piece):
        return next(i for i, h in enumerate(HOPS) if h[1] == dst and h[3] == piece)

    def send(*names):
        for dst, piece in names:
            for side in (0, 1):
                go(hop(side, index(dst, piece)))

    def arrived(*names, sides=(0, 1)):
        for dst, piece in names:
            for side in sides:
                hop(side, index(dst, piece)).wait_recv()

    def to_sibling(slot, kind):
        ref = xt if kind == "T" else xs
        k = 0 if kind == "T" else 1
        return remote(
            ref.at[pl.ds(2 * POS[slot] * B, B), :], ref.at[pl.ds((2 * POS[slot] + 1) * B, B), :],
            sib_send.at[k, slot], sib_recv.at[k, slot], sibling,
        )

    def share(kind, *slots):
        for slot in slots:
            go(to_sibling(slot, kind))

    def shared(kind, *slots):
        for slot in slots:
            to_sibling(slot, kind).wait_recv()

    def logits(mat, rows, cols):
        left, right, out = ((is_, xs, es), (it, xt, et))[mat]
        for c in range(cols[0] * 2 * B, cols[1] * 2 * B, 2 * B):
            r = rows[0] * B
            while r < rows[1] * B:
                n = min(512, rows[1] * B - r)
                e = jnp.exp2(dot_nt(left[r : r + n, :], right[c : c + 256, :]) * (LOGIT_SCALE * LOG2E))
                out[r : r + n, c : c + 256] = e
                row_acc[mat, r : r + n, :] += e[:, 0:128] + e[:, 128:256]
                col_acc[mat, :, c : c + 256] += jnp.sum(e.reshape(n // 8, 8, 256), axis=0)
                r += n

    loads[0].wait()
    loads[1].wait()
    normalize(si_ref, is_, i0, 0, B)
    normalize(st_ref, xs, t0, 0, B)
    loads[2].wait()
    loads[3].wait()
    normalize(ti_ref, it, i0, 0, B)
    normalize(tt_ref, xt, t0, 0, B)
    pl.semaphore_wait(barrier, 7)
    send((1, "S"), (3, "T0"), (2, "T0"), (1, "T0"), (3, "T1"), (2, "T1"), (3, "S"), (2, "S"))
    share("T", 0)
    share("S", 0)

    @segment
    def _():
        row_acc[...] = jnp.zeros_like(row_acc)
        col_acc[...] = jnp.zeros_like(col_acc)

    arrived((3, "T0"))
    send((6, "T0"), (4, "T0"))
    arrived((1, "S"))
    share("S", 1)
    arrived((2, "T0"), (2, "T1"))
    send((5, "T1"), (4, "T1"))
    arrived((3, "T1"))
    send((6, "T1"), (1, "T1"))
    arrived((1, "T0"))
    send((5, "T0"))
    share("T", 2, 3)
    arrived((3, "S"))
    send((4, "S"))
    arrived((2, "S"))
    share("S", 2, 3)
    arrived((6, "T0"))
    send((7, "T0"), (6, "S"))
    shared("T", 0, 2, 3)

    @segment
    def _():
        logits(1, (0, 3), (0, 3))

    arrived((4, "T0"), (4, "T1"))
    share("T", 4)
    arrived((5, "T1"))
    send((7, "T1"), (5, "S"))
    shared("S", 0, 1, 2, 3)

    @segment
    def _():
        logits(0, (0, 3), (0, 3))
        logits(0, (0, 3), (4, 5))

    shared("T", 4)

    @segment
    def _():
        logits(1, (0, 3), (3, 4))
        logits(1, (3, 4), (0, 4))

    arrived((4, "S"))
    send((7, "S"))
    share("S", 4)
    arrived((5, "T0"), (6, "T1"))
    share("T", 5, 6)

    @segment
    def _():
        logits(1, (6, 8), (0, 4))

    shared("T", 5, 6)

    @segment
    def _():
        logits(1, (0, 4), (6, 8))
        logits(1, (6, 8), (6, 8))

    for slot, pieces in ((1, ("T1",)), (7, ("T0", "T1"))):
        arrived(*((slot, piece) for piece in pieces), sides=(1,))
        share("T", slot)
    arrived((1, "T1"), (7, "T0"), (7, "T1"), sides=(0,))
    shared("S", 4)

    @segment
    def _():
        logits(0, (3, 5), (0, 5))
        logits(0, (0, 3), (3, 4))
        logits(1, (4, 6), (0, 4))
        logits(1, (4, 6), (6, 8))

    shared("T", 1, 7)

    @segment
    def _():
        logits(1, (0, 4), (4, 6))

    for slot in (5, 6, 7):
        arrived((slot, "S"), sides=(1,))
        share("S", slot)

    @segment
    def _():
        logits(1, (4, 8), (4, 6))

    arrived((5, "S"), (6, "S"), (7, "S"), sides=(0,))

    def sum_sib(mat):
        return remote(tsum.at[mat], tsum_sib.at[mat], sum_send.at[mat, 14], sum_recv.at[mat, 14], sibling)

    def sum_copy(mat, side, slot):
        back = minus(0, slot) - 1
        return remote(
            (isum, csum)[side].at[mat], (isum_in, tsum_in)[side].at[mat, back],
            sum_send.at[mat, side * 7 + slot - 1], sum_recv.at[mat, side * 7 + back], peers[side](*SLOTS[slot]),
        )

    def sum_from(mat, side, slot):
        return remote(
            (isum, csum)[side].at[mat], (isum_in, tsum_in)[side].at[mat, slot - 1],
            sum_send.at[mat, side * 7 + slot - 1], sum_recv.at[mat, side * 7 + slot - 1], peers[side](*SLOTS[slot]),
        )

    def sums_out(mat):
        @segment
        def _():
            for b in range(2 * N):
                tsum[mat, b : b + 1, :] = jnp.sum(col_acc[mat, :, b * B : (b + 1) * B], axis=0, keepdims=True)

        go(sum_sib(mat))

        @segment
        def _():
            for p in range(N):
                isum[mat, p : p + 1, :] = jnp.sum(row_acc[mat, p * B : (p + 1) * B, :].T, axis=0, keepdims=True)

        for slot in range(N - 1, 0, -1):
            go(sum_copy(mat, 0, slot))

    def text_sums_out(mat):
        sum_sib(mat).wait_recv()

        @segment
        def _():
            for p in range(N):
                r = 2 * p
                csum[mat, r : r + 1, :] = tsum[mat, r : r + 1, :] + tsum_sib[mat, r + 1 : r + 2, :]
                csum[mat, r + 1 : r + 2, :] = tsum[mat, r + 1 : r + 2, :] + tsum_sib[mat, r : r + 1, :]

        for slot in range(N - 1, 0, -1):
            go(sum_copy(mat, 1, slot))

    half = 0.5 * LOGIT_SCALE

    def sums_in(mat):
        for slot in range(1, N):
            sum_from(mat, 0, slot).wait_recv()

        @segment
        def _():
            for t in range(N):
                total = isum[mat, POS[t] : POS[t] + 1, :]
                for e in range(1, N):
                    q = POS[minus(t, e)]
                    total = total + isum_in[mat, e - 1, q : q + 1, :]
                row_inv[mat, POS[t] * B : (POS[t] + 1) * B, :] = jnp.broadcast_to(half / total, (B, B)).T

        for slot in range(1, N):
            sum_from(mat, 1, slot).wait_recv()

        @segment
        def _():
            for t in range(N):
                for par in (0, 1):
                    r = 2 * POS[t] + par
                    total = csum[mat, r : r + 1, :]
                    for e in range(1, N):
                        q = 2 * POS[minus(t, e)] + par
                        total = total + tsum_in[mat, e - 1, q : q + 1, :]
                    col_inv[mat, :, r * B : (r + 1) * B] = jnp.broadcast_to(half / total, (8, B))

    def weighted(mat, e, r, c):
        factor = row_inv[mat, r : r + 64, :].reshape(8, 8, B) + col_inv[mat, :, c : c + B][None]
        return e[r : r + 64, c : c + B].reshape(8, 8, B) * factor

    sums_out(1)

    @segment
    def _():
        logits(0, (5, 8), (0, 5))

    text_sums_out(1)
    shared("S", 5, 6, 7)

    @segment
    def _():
        logits(0, (0, 8), (5, 8))

    gathered = len(started)
    sums_out(0)

    @segment
    def _():
        for p in range(N):
            ist[:, p * B : (p + 1) * B] = is_[p * B : (p + 1) * B, :].T

    text_sums_out(0)
    drain(gathered)
    sums_in(1)

    @segment
    def _():
        for r in range(0, N * B, 64):
            for c in range(0, 2 * N * B, B):
                et[r : r + 64, c : c + B] = weighted(1, et, r, c).reshape(64, B)

    sums_in(0)

    def weights(rows, cols):
        for r in range(rows[0] * B, rows[1] * B, 64):
            for c in range(cols[0] * 2 * B, cols[1] * 2 * B, B):
                term = weighted(0, es, r, c).reshape(64, B) - et[r : r + 64, c : c + B]
                w[r : r + 64, c : c + B] = term.astype(BF16)

    def halves(slot):
        return (0, 1) if slot in HALVED else (None,)

    def span(side, part):
        rows = (B, 512)[side]
        return (0, rows) if part is None else (part * rows // 2, rows // 2)

    def grad_copy(side, slot, part):
        first, rows = span(side, part)
        return remote(
            (di_out, dt_out)[side].at[slot, pl.ds(first, rows), :], (di_in, dt_in)[side].at[slot, pl.ds(first, rows), :],
            grad_send.at[side, slot, part or 0], grad_recv.at[side, slot, part or 0], peers[side](*GRAD_TO[slot]),
        )

    def grad_sib(slot):
        return remote(
            dt_other.at[slot], dt_sib.at[slot], grad_sib_send.at[slot], grad_sib_recv.at[slot], sibling
        )

    def text_terms(*slots):
        for slot in slots:
            c = 2 * POS[slot] * B
            out = jnp.dot(ist[...], w[:, c : c + 2 * B], preferred_element_type=F32)
            dt_keep[slot] = out[:, 0:B]
            dt_other[slot] = out[:, B : 2 * B].astype(BF16)

    def text_share(*slots):
        for slot in slots:
            go(grad_sib(slot))

    def total_of(side, slot, part=None):
        first, rows = span(side, part)
        at = pl.ds(first, rows)
        if side == 0:
            total = di_keep[slot, at, :]
        else:
            total = dt_keep[slot, at, :] + dt_sib[slot, at, :].astype(F32)
        for source in SINKS.get(slot, ()):
            for half_of in halves(source) if part is None else (part,):
                grad_copy(side, source, half_of).wait_recv()
            total = total + (di_in, dt_in)[side][source, at, :].astype(F32)
        return total

    def grad_sum_send(side, slot, part=None):
        first, rows = span(side, part)
        (di_out, dt_out)[side][slot, pl.ds(first, rows), :] = total_of(side, slot, part).astype(BF16)
        go(grad_copy(side, slot, part))

    def text_send(*slots):
        for slot in slots:
            grad_sib(slot).wait_recv()
            for part in halves(slot):
                grad_sum_send(1, slot, part)

    def image_terms(p0, p1):
        out = jnp.dot(w[p0 * B : p1 * B, :], xs[...], preferred_element_type=F32)
        for p in range(p0, p1):
            part = out[(p - p0) * B : (p - p0 + 1) * B, :]
            if ORDER[p] in SINKS:
                di_keep[ORDER[p]] = part
            else:
                di_out[ORDER[p]] = part.astype(BF16)

    def image_send(*slots):
        for slot in slots:
            for part in halves(slot):
                go(grad_copy(0, slot, part))

    summed = len(started)

    @segment
    def _():
        weights((0, 8), (6, 8))
        text_terms(5, 6)

    text_share(5, 6)

    @segment
    def _():
        weights((0, 8), (5, 6))
        text_terms(7)

    text_share(7)

    @segment
    def _():
        weights((5, 8), (0, 5))
        image_terms(5, 8)

    image_send(7, 5, 6)
    text_send(5, 6, 7)

    @segment
    def _():
        weights((0, 5), (1, 3))
        text_terms(2, 3)

    text_share(2, 3)

    @segment
    def _():
        weights((0, 5), (0, 1))
        weights((0, 5), (3, 5))
        image_terms(1, 3)

    image_send(2, 3)

    @segment
    def _():
        text_terms(4, 1)

    text_share(4, 1)
    text_send(2, 3)

    @segment
    def _():
        image_terms(3, 5)

    drain(summed)
    shared_terms = len(started)
    grad_sum_send(0, 4)
    text_send(4)
    grad_sum_send(0, 1)
    text_send(1)

    @segment
    def _():
        text_terms(0)

    text_share(0)

    @segment
    def _():
        image_terms(0, 1)

    grad_sib(0).wait_recv()
    drain(shared_terms)

    gi_ref[...] = total_of(0, 0)
    gt_ref[...] = total_of(1, 0).T

    drain(len(started))


def finish_kernel(si_ref, st_ref, di_ref, dt_ref, gi_hbm, gt_hbm, grads, sems):
    copies = [pltpu.make_async_copy(grads.at[i], out, sems.at[i]) for i, out in enumerate((gi_hbm, gt_hbm))]
    for i, (raw, total) in enumerate(((si_ref, di_ref), (st_ref, dt_ref))):
        norm, inverse = unit_rows(raw[...])
        direction = total[...]
        grads[i] = inverse * (direction - norm * jnp.sum(norm * direction, axis=1, keepdims=True))
        copies[i].start()
    for copy in copies:
        copy.wait()


def per_device(teacher_image, student_image, teacher_text, student_text):
    vmem, anywhere = pl.BlockSpec(memory_space=pltpu.VMEM), pl.BlockSpec(memory_space=pl.ANY)
    dma = pltpu.SemaphoreType.DMA
    directions = pl.pallas_call(
        kernel,
        out_shape=(pltpu.VMEM((B, 512), F32), pltpu.VMEM((B, 512), F32)),
        in_specs=[anywhere] * 4,
        out_specs=(vmem, vmem),
        scratch_shapes=[
            pltpu.VMEM((B, 1024), BF16),
            pltpu.VMEM((B, 512), BF16),
            pltpu.VMEM((B, 1024), BF16),
            pltpu.VMEM((B, 512), BF16),
            pltpu.VMEM((N * B, 1024), BF16),
            pltpu.VMEM((N * B, 512), BF16),
            pltpu.VMEM((2 * N * B, 1024), BF16),
            pltpu.VMEM((2 * N * B, 512), BF16),
            pltpu.VMEM((N * B, 2 * N * B), F32),
            pltpu.VMEM((N * B, 2 * N * B), F32),
            pltpu.VMEM((N * B, 2 * N * B), BF16),
            pltpu.VMEM((512, N * B), BF16),
            pltpu.VMEM((2, N * B, B), F32),
            pltpu.VMEM((2, 8, 2 * N * B), F32),
            pltpu.VMEM((2, N * B, B), F32),
            pltpu.VMEM((2, 8, 2 * N * B), F32),
            pltpu.VMEM((2, N, B), F32),
            pltpu.VMEM((2, 7, N, B), F32),
            pltpu.VMEM((2, 2 * N, B), F32),
            pltpu.VMEM((2, 2 * N, B), F32),
            pltpu.VMEM((2, 2 * N, B), F32),
            pltpu.VMEM((2, 7, 2 * N, B), F32),
            pltpu.VMEM((N, B, 512), F32),
            pltpu.VMEM((N, B, 512), BF16),
            pltpu.VMEM((N, B, 512), BF16),
            pltpu.VMEM((N, 512, B), F32),
            pltpu.VMEM((N, 512, B), BF16),
            pltpu.VMEM((N, 512, B), BF16),
            pltpu.VMEM((N, 512, B), BF16),
            pltpu.VMEM((N, 512, B), BF16),
            dma((4,)),
            dma((2, N_HOPS)),
            dma((2, N_HOPS)),
            dma((2, N)),
            dma((2, N)),
            dma((2, 15)),
            dma((2, 15)),
            dma((2, N, 2)),
            dma((2, N, 2)),
            dma((N,)),
            dma((N,)),
        ],
        compiler_params=pltpu.CompilerParams(
            collective_id=0, has_side_effects=True, vmem_limit_bytes=60 << 20
        ),
        cost_estimate=pl.CostEstimate(flops=10_737_418_240, bytes_accessed=1 << 20, transcendentals=1 << 22),
    )(teacher_image, student_image, teacher_text, student_text)
    out = jax.ShapeDtypeStruct((B, 512), F32)
    return pl.pallas_call(
        finish_kernel,
        out_shape=(out, out),
        in_specs=[vmem] * 4,
        out_specs=(anywhere, anywhere),
        scratch_shapes=[pltpu.VMEM((2, B, 512), F32), dma((2,))],
        compiler_params=pltpu.CompilerParams(vmem_limit_bytes=4 << 20),
    )(student_image, student_text, *directions)


def solution(mesh):
    spec = P(("grp", "row", "col"), None)
    return jax.shard_map(
        per_device, mesh=mesh, in_specs=(spec,) * 4, out_specs=(spec, spec), check_vma=False
    )
```
